32 devices in a mesh: cuts: 2 (over y), mode: 4 (over z), group: 2 (over x), batch: 2 (over core).
Axes of the slice: x: 2, y: 2, z: 4, core: 2. Of those that a mesh axis runs over, the one named last changes fastest.
Arguments:
- stem_slice: bfloat16 [2, 4, 16384, 128], P(None, ('cuts', 'batch'), ('mode', 'group')), parts along dimension 1, may hold values from -6 to 6
- column_branch: bfloat16 [2, 128, 128], replicated, may hold values from -0.375 to 0.375
- row_branch: bfloat16 [2, 128, 128], replicated, may hold values from -0.375 to 0.375
- mode_branch: bfloat16 [2, 128, 128], replicated, may hold values from -0.375 to 0.375
- final_branch: bfloat16 [2, 1024, 128], replicated, may hold values from -0.125 to 0.125
- row_labels: int32 [128], replicated, may hold values from 0 to 127, each once
- mode_labels: int32 [128], replicated, may hold values from 0 to 127, each once
- requests: int32 [2, 232], P('batch', ('mode', 'group')), may hold values from 0 to 2047, as said below
Outputs:
- amplitudes: bfloat16 [2, 4, 232, 128], P(None, ('cuts', 'batch'), ('mode', 'group')), parts along dimension 1
The draws below stay inside these ranges and needn't reach their ends.
There are 2 independent parts, one for each index of `cuts`. The reference program is written for one: setup_inputs(seed, part) draws one part's arguments, and reference() takes and returns one part's arrays. A program takes and returns all parts, laid end to end along the dimension named above; an argument that names none is the same for every part. Nothing has to cross between parts.
Inputs may be any that keep to these rules, and one draw needn't show every extreme that they name: `requests`: within each set, each device's 29 entries name rows of its own batch slice; at most 8 of one device's entries name rows held by one device (index divided by 256), and some device of each set is named exactly 8 times by every device of the set. `row_labels`: a permutation. `mode_labels`: a permutation.
All inputs are finite; a program needn't handle non-finite values.
Results may differ from the reference program's by a relative error of at most 0.0064.
Values may be sent and summed in bfloat16 or wider, within the bound.
A program may use at most 64 MiB of HBM per device.

```python
import jax
import jax.numpy as jnp
from jax import lax

COLUMNS = 128
BRANCH_ORDER = 128
OUT_WIDTH = 128
LOCAL_ROWS = 2048
CAPACITY = 8
LOW_COUNT = 3
OWNER_SETS = 2
PEER_COUNT = 8
SUB_ROWS = 16
BLOCKS = 16
ROW_LENGTH = 1024
STEM_ROWS = 256
HOT_PEERS = 1
REQUESTS = 29


def one_owner_set(set_key):
    key_list = jax.random.split(set_key, 4)
    hot_peer = jax.random.randint(key_list[0], (), 0, PEER_COUNT)
    peer_ids = jnp.arange(PEER_COUNT, dtype=jnp.int32)

    def peer_order(order_key):
        scores = jax.random.permutation(order_key, PEER_COUNT).astype(jnp.int32)
        scores = jnp.where(peer_ids == hot_peer, -1, scores)
        return jnp.argsort(scores, stable=True).astype(jnp.int32)
    orders = jax.vmap(peer_order)(jax.random.split(key_list[1], PEER_COUNT))
    position = jnp.arange(REQUESTS, dtype=jnp.int32)
    head_size = HOT_PEERS * CAPACITY
    tail_pos = jnp.maximum(position - head_size, 0)
    slot_peer = jnp.where(position < head_size, position // CAPACITY, HOT_PEERS + tail_pos // LOW_COUNT)
    slot_index = jnp.where(position < head_size, position % CAPACITY, tail_pos % LOW_COUNT)
    target = jnp.take(orders, slot_peer, axis=1)
    local_rows = jax.random.randint(key_list[2], (PEER_COUNT, REQUESTS), 0, STEM_ROWS)
    local_rows = jnp.where((target == PEER_COUNT - 1) & (slot_index[None, :] == 0), STEM_ROWS - 1, local_rows)
    local_rows = jnp.where((target == 0) & (slot_index[None, :] == 0), 0, local_rows)
    row_ids = target * STEM_ROWS + local_rows

    def shuffle(shuffle_key, id_list):
        return jnp.take(id_list, jax.random.permutation(shuffle_key, REQUESTS))
    row_ids = jax.vmap(shuffle)(jax.random.split(key_list[3], PEER_COUNT), row_ids)
    return row_ids.reshape(-1).astype(jnp.int32)


def draw_requests(key, part):
    set_keys = jax.random.split(jax.random.fold_in(key, 7331), OWNER_SETS)
    return jax.vmap(one_owner_set)(set_keys)


def block_levels(stream_key, extent, pieces, least, largest):
    factor_of = 1.0
    for dim, parts in pieces:
        steps = jax.random.uniform(jax.random.fold_in(jax.random.fold_in(stream_key, 6), dim), (parts,), jnp.float32, least / len(pieces), largest / len(pieces))
        factor_of = factor_of * jnp.repeat(jnp.exp(steps), extent[dim] // parts).reshape((-1,) + (1,) * (len(extent) - 1 - dim))
    return factor_of


def scatter_about(stream_key, dims, width, limit, cuts=(), kind=jnp.bfloat16):
    array = width * jax.random.normal(stream_key, dims, jnp.float32)
    if cuts:
        array = array * block_levels(stream_key, dims, cuts, -0.22, 0.18)
    return jnp.clip(array, -limit, limit).astype(kind)


def setup_inputs(seed: int = 0, part: int = 0) -> dict:
    key_of = jax.random.split(jax.random.key(seed), 9)
    own_keys = jax.random.split(jax.random.fold_in(key_of[8], part), 9)
    return {
        "stem_slice": scatter_about(own_keys[0], (2, OWNER_SETS, PEER_COUNT * LOCAL_ROWS, COLUMNS), 1.0, 6.0, ((1, 2), (2, 8))),
        "column_branch": scatter_about(key_of[1], (2, COLUMNS, COLUMNS), (2 * COLUMNS) ** -0.5, 0.375),
        "row_branch": scatter_about(key_of[2], (2, COLUMNS, COLUMNS), (2 * COLUMNS) ** -0.5, 0.375),
        "mode_branch": scatter_about(key_of[3], (2, BRANCH_ORDER, BRANCH_ORDER), (2 * BRANCH_ORDER) ** -0.5, 0.375),
        "final_branch": scatter_about(key_of[4], (2, ROW_LENGTH, OUT_WIDTH), (2 * ROW_LENGTH) ** -0.5, 0.125),
        "row_labels": jax.random.permutation(key_of[5], COLUMNS).astype(jnp.int32),
        "mode_labels": jax.random.permutation(key_of[6], BRANCH_ORDER).astype(jnp.int32),
        "requests": draw_requests(jax.random.fold_in(key_of[8], 71), part),
    }


def matmul_wide(left_matrix, right_matrix):
    return jnp.dot(left_matrix, right_matrix, preferred_element_type=jnp.float32)


def complex_product(operand, weight):
    real_part = matmul_wide(operand[0], weight[0]) - matmul_wide(operand[1], weight[1])
    imag_part = matmul_wide(operand[0], weight[1]) + matmul_wide(operand[1], weight[0])
    return jnp.stack([real_part, imag_part])


def reference(stem_slice, column_branch, row_branch, mode_branch, final_branch, row_labels, mode_labels, requests):
    outputs = []
    for owner_set in range(OWNER_SETS):
        whole_stem = stem_slice[:, owner_set].reshape(2, PEER_COUNT, LOCAL_ROWS, COLUMNS).transpose(1, 0, 2, 3)

        def first_section(block):
            column_mixed = complex_product(block, column_branch).astype(jnp.bfloat16)
            grouped = column_mixed.reshape(2, LOCAL_ROWS // COLUMNS, COLUMNS, COLUMNS)
            grouped = jnp.take(grouped, row_labels, axis=2).transpose(0, 1, 3, 2)
            row_mixed = complex_product(grouped, row_branch).transpose(0, 1, 3, 2)
            return row_mixed.astype(jnp.bfloat16).reshape(2, LOCAL_ROWS, COLUMNS)

        row_mixed = lax.map(first_section, whole_stem)
        swapped = row_mixed.reshape(PEER_COUNT, 2, PEER_COUNT, BLOCKS, SUB_ROWS, COLUMNS).transpose(2, 1, 0, 3, 4, 5)

        def second_section(block):
            gathered = block.transpose(0, 2, 4, 1, 3).reshape(2, BLOCKS, COLUMNS, BRANCH_ORDER)
            gathered = jnp.take(gathered, mode_labels, axis=3)
            mode_mixed = complex_product(gathered, mode_branch).transpose(0, 1, 3, 2)
            return mode_mixed.astype(jnp.bfloat16).reshape(2, STEM_ROWS, ROW_LENGTH)

        stem_rows = lax.map(second_section, swapped).transpose(1, 0, 2, 3).reshape(2, PEER_COUNT * STEM_ROWS, ROW_LENGTH)
        fetched = jnp.take(stem_rows, requests[owner_set], axis=1)
        outputs.append(complex_product(fetched, final_branch).astype(jnp.bfloat16))
    return jnp.stack(outputs, axis=1)
```

```python
import functools

import jax
import jax.numpy as jnp
from jax import lax
from jax.experimental import pallas as pl
from jax.experimental.pallas import tpu as pltpu
from jax.sharding import PartitionSpec as P

CAPACITY = 8
TILE = 8
ROWS_STEP = 2

F32 = jnp.float32
BF16 = jnp.bfloat16


def dot(left, right):
    return jnp.dot(left, right, preferred_element_type=F32)


def dot_t(left, right):
    return lax.dot_general(left, right, (((1,), (1,)), ((), ())), preferred_element_type=F32)


def iota(shape, dim):
    return lax.broadcasted_iota(jnp.int32, shape, dim)


def complex_rows(real, imag, axis):
    return jnp.concatenate([real, -imag], axis), jnp.concatenate([imag, real], axis)


def fused_kernel(
    mode_size,
    group_size,
    stem_hbm,
    column_hbm,
    row_hbm,
    mode_hbm,
    final_hbm,
    row_labels_hbm,
    mode_labels_hbm,
    requests_hbm,
    out_ref,
    stem,
    column,
    row,
    mode,
    final,
    row_labels,
    mode_labels,
    wanted,
    asked,
    spread,
    picked,
    coeffs,
    partial,
    outgoing,
    incoming,
    load_sem,
    stem_sem,
    ask_send,
    ask_recv,
    give_send,
    give_recv,
):
    peers = mode_size * group_size
    row_count, width = stem.shape[1], stem.shape[2]
    row_order = row.shape[1]
    order = mode.shape[1]
    sub = order // peers
    heads = row_order // sub
    groups = row_count // row_order
    length = final.shape[1]
    fold = length // width
    out_width = final.shape[2]
    count = wanted.shape[1]
    padded = outgoing.shape[1]
    total = peers * padded
    blocks = row_count // sub
    row_blocks = order // fold
    terms = 2 * sub
    span = terms * TILE

    mode_index = lax.axis_index("mode")
    group_index = lax.axis_index("group")
    me = mode_index * group_size + group_index

    def device(offset):
        peer = lax.rem(me + offset, peers)
        return {"mode": peer // group_size, "group": lax.rem(peer, group_size)}

    barrier = pltpu.get_barrier_semaphore()
    for offset in range(1, peers):
        pl.semaphore_signal(
            barrier, inc=1, device_id=device(offset), device_id_type=pl.DeviceIdType.MESH
        )

    small = [
        pltpu.make_async_copy(source, target, load_sem.at[index])
        for index, (source, target) in enumerate(
            (
                (requests_hbm, wanted),
                (column_hbm, column),
                (row_hbm, row),
                (row_labels_hbm, row_labels),
                (mode_hbm, mode),
                (mode_labels_hbm, mode_labels),
                (final_hbm, final),
            )
        )
    ]
    step_rows = ROWS_STEP * row_order
    stem_loads = [
        pltpu.make_async_copy(
            stem_hbm.at[:, 0, pl.ds(step * step_rows, step_rows), :],
            stem.at[:, pl.ds(step * step_rows, step_rows), :],
            stem_sem.at[step],
        )
        for step in range(groups // ROWS_STEP)
    ]
    for load in small[:-1]:
        load.start()
    for load in stem_loads:
        load.start()
    small[-1].start()

    small[0].wait()
    asked[0:1, :] = jnp.zeros((1, width), jnp.int32)
    asked[0:1, 0:count] = wanted[...]
    pl.semaphore_wait(barrier, peers - 1)
    asks = [
        pltpu.make_async_remote_copy(
            src_ref=asked.at[pl.ds(0, 1), :],
            dst_ref=asked.at[pl.ds(offset, 1), :],
            send_sem=ask_send.at[offset],
            recv_sem=ask_recv.at[offset],
            device_id=device(offset),
            device_id_type=pl.DeviceIdType.MESH,
        )
        for offset in range(1, peers)
    ]
    for ask in asks:
        ask.start()

    for load in small[1:4]:
        load.wait()
    column_real, column_imag = complex_rows(column[0], column[1], 0)
    column_table = jnp.concatenate([column_real, column_imag], 1)
    chosen = (iota((row_order, row_order), 0) == row_labels[...]).astype(BF16)
    order_out = iota((row_order, row_order), 0)
    order_in = iota((row_order, row_order), 1)
    swap_rows = (
        order_in == lax.rem(order_out, heads) * sub + lax.div(order_out, heads)
    ).astype(BF16)
    row_real = dot_t(swap_rows, dot(chosen, row[0]).astype(BF16)).astype(BF16)
    row_imag = dot_t(swap_rows, dot(chosen, row[1]).astype(BF16)).astype(BF16)
    row_table = jnp.concatenate(complex_rows(row_real, row_imag, 1), 0)

    for step in range(groups // ROWS_STEP):
        stem_loads[step].wait()
        rows = pl.ds(step * step_rows, step_rows)
        operand = jnp.concatenate([stem[0, rows, :], stem[1, rows, :]], 1)
        mixed = dot(operand, column_table).astype(BF16)
        pieces = []
        for index in range(ROWS_STEP):
            piece = mixed[index * row_order : (index + 1) * row_order]
            pieces.append(jnp.concatenate([piece[:, :width], piece[:, width:]], 0))
        result = dot(row_table, jnp.concatenate(pieces, 1))
        for index in range(ROWS_STEP):
            first = (step * ROWS_STEP + index) * heads
            spread[:, first : first + heads, :] = result[
                :, index * width : (index + 1) * width
            ].reshape(terms, heads, width)

    for load in small[4:6]:
        load.wait()
    own = (iota((sub, order), 0) + me * sub == mode_labels[...]).astype(BF16)
    mode_real, mode_imag = dot(own, mode[0]), dot(own, mode[1])
    repeat = (lax.div(iota((span, terms), 0), TILE) == iota((span, terms), 1)).astype(BF16)
    mode_table = jnp.concatenate(
        [dot(repeat, half.astype(BF16)) for half in complex_rows(mode_real, mode_imag, 0)], 0
    ).astype(BF16)

    for ask in asks:
        ask.wait()
    ids = asked[...]
    block_ids = jnp.transpose(lax.div(ids, row_blocks).astype(F32))
    order_ids = jnp.transpose((lax.rem(ids, row_blocks) * fold).astype(F32))

    def column_of(values, lanes):
        return jnp.concatenate(
            [
                jnp.broadcast_to(values[:padded, slot : slot + 1], (padded, lanes))
                for slot in range(peers)
            ],
            0,
        )

    lane = iota((total, blocks), 1).astype(F32)
    pick = (column_of(block_ids, blocks) == lane).astype(BF16)
    for term in range(0, terms, 2):
        pair = jnp.concatenate([spread[term], spread[term + 1]], 1).astype(BF16)
        found = dot(pick, pair)
        picked[term] = found[:, :width]
        picked[term + 1] = found[:, width:]

    order_column = column_of(order_ids, order)
    lane = iota((total, order), 1).astype(F32)
    same = lax.rem(iota((total, 2 * span), 0), TILE) == lax.rem(iota((total, 2 * span), 1), TILE)
    for index in range(fold):
        at = (order_column + float(index) == lane).astype(BF16)
        values = jnp.where(same, dot_t(at, mode_table), 0.0)
        coeffs[index] = values[:, :span]
        coeffs[fold + index] = values[:, span:]

    for tile in range(total // TILE):
        rows = pl.ds(tile * TILE, TILE)
        left = coeffs[:, rows, :].reshape(2 * fold * TILE, span).astype(BF16)
        right = picked[:, rows, :].reshape(span, width).astype(BF16)
        partial[:, rows, :] = dot(left, right).reshape(2 * fold, TILE, width)

    small[6].wait()
    halves = []
    for half in range(2):
        halves.append(
            jnp.concatenate(
                [partial[half * fold + index].astype(BF16) for index in range(fold)], 1
            )
        )
    products = dot(halves[0], jnp.concatenate([final[0], final[1]], 1)) + dot(
        halves[1], jnp.concatenate([-final[1], final[0]], 1)
    )
    outgoing[...] = products.reshape(peers, padded, 2 * out_width).astype(BF16)

    gives = [
        pltpu.make_async_remote_copy(
            src_ref=outgoing.at[offset],
            dst_ref=incoming.at[offset],
            send_sem=give_send.at[offset],
            recv_sem=give_recv.at[offset],
            device_id=device(peers - offset),
            device_id_type=pl.DeviceIdType.MESH,
        )
        for offset in range(1, peers)
    ]
    for give in gives:
        give.start()
    answer = products[:padded]
    for offset, give in enumerate(gives, 1):
        give.wait_recv()
        answer = answer + incoming[offset].astype(F32)
    answer = answer.astype(out_ref.dtype)
    out_ref[0, 0] = answer[:count, :out_width]
    out_ref[1, 0] = answer[:count, out_width:]
    for give in gives:
        give.wait_send()


def fused(mode_size, group_size, padded, arguments):
    stem_slice, column, row, mode, final, row_labels, mode_labels, requests = arguments
    peers = mode_size * group_size
    row_count, width = stem_slice.shape[2:]
    order = mode.shape[1]
    sub = order // peers
    fold = final.shape[1] // width
    out_width = final.shape[2]
    count = requests.shape[1]
    total = peers * padded
    terms = 2 * sub
    span = terms * TILE
    steps = row_count // row.shape[1] // ROWS_STEP
    row_labels = row_labels.reshape(1, -1)
    mode_labels = mode_labels.reshape(1, -1)
    dma = pltpu.SemaphoreType.DMA
    return pl.pallas_call(
        functools.partial(fused_kernel, mode_size, group_size),
        out_shape=jax.ShapeDtypeStruct((2, 1, count, out_width), BF16),
        in_specs=[pl.BlockSpec(memory_space=pltpu.HBM)] * 8,
        out_specs=pl.BlockSpec(memory_space=pltpu.VMEM),
        scratch_shapes=[
            pltpu.VMEM((2, row_count, width), BF16),
            pltpu.VMEM(column.shape, BF16),
            pltpu.VMEM(row.shape, BF16),
            pltpu.VMEM(mode.shape, BF16),
            pltpu.VMEM(final.shape, BF16),
            pltpu.VMEM(row_labels.shape, jnp.int32),
            pltpu.VMEM(mode_labels.shape, jnp.int32),
            pltpu.VMEM(requests.shape, jnp.int32),
            pltpu.VMEM((peers, width), jnp.int32),
            pltpu.VMEM((terms, row_count // sub, width), F32),
            pltpu.VMEM((terms, total, width), F32),
            pltpu.VMEM((2 * fold, total, span), F32),
            pltpu.VMEM((2 * fold, total, width), F32),
            pltpu.VMEM((peers, padded, 2 * out_width), BF16),
            pltpu.VMEM((peers, padded, 2 * out_width), BF16),
            dma((7,)),
            dma((steps,)),
            dma((peers,)),
            dma((peers,)),
            dma((peers,)),
            dma((peers,)),
        ],
        compiler_params=pltpu.CompilerParams(
            collective_id=0, has_side_effects=True, vmem_limit_bytes=48 * 1024 * 1024
        ),
    )(stem_slice, column, row, mode, final, row_labels, mode_labels, requests)


def complex_table(weight):
    real_part = weight[0]
    imag_part = weight[1]
    return jnp.stack([jnp.stack([real_part, imag_part], 1), jnp.stack([-imag_part, real_part], 1)])


def relabel(weight, labels):
    label_count = labels.shape[0]
    onehot = (labels[:, None] == jnp.arange(label_count, dtype=jnp.int32)[None, :]).astype(
        jnp.float32
    )
    relabelled = jnp.einsum(
        "ji,zjn->zin", onehot, weight.astype(jnp.float32), precision=lax.Precision.HIGHEST
    )
    return complex_table(relabelled.astype(jnp.bfloat16))


def swapped(
    stem_slice,
    column_branch,
    row_branch,
    mode_branch,
    final_branch,
    row_labels,
    mode_labels,
    requests,
):
    local_block = stem_slice[:, 0]
    row_count = local_block.shape[1]
    col_width = local_block.shape[2]
    first_mixed = jnp.einsum(
        "zlc,zcwk->wlk",
        local_block,
        complex_table(column_branch),
        preferred_element_type=jnp.float32,
    ).astype(jnp.bfloat16)
    grouped = first_mixed.reshape(2, row_count // col_width, col_width, col_width)
    second = jnp.einsum(
        "zgjc,zjwk->wgkc",
        grouped,
        relabel(row_branch, row_labels),
        preferred_element_type=jnp.float32,
    ).astype(jnp.bfloat16)
    peer_count = lax.axis_size(("mode", "group"))
    order_size = mode_branch.shape[1]
    sub_rows = order_size // peer_count
    blocks = row_count // order_size
    mode_table = relabel(mode_branch, mode_labels).reshape(2, peer_count, sub_rows, 2, order_size)
    shaped = second.reshape(2, peer_count, blocks, sub_rows, col_width)
    mode_mixed = jnp.einsum(
        "zqhsc,zqswk->whkc",
        lax.all_to_all(shaped, ("mode", "group"), split_axis=1, concat_axis=1, tiled=True),
        mode_table,
        preferred_element_type=jnp.float32,
    ).astype(jnp.bfloat16)
    stem_rows = mode_mixed.reshape(2, row_count // 8, 8 * col_width)
    row_total = stem_rows.shape[1]
    wanted = requests[0]
    owner_index = wanted // row_total
    row_index = wanted - owner_index * row_total
    peer_ids = jnp.arange(peer_count, dtype=jnp.int32)
    onehot = (owner_index[:, None] == peer_ids[None, :]).astype(jnp.int32)
    slot_rank = jnp.sum((jnp.cumsum(onehot, axis=0) - onehot) * onehot, axis=1)
    flat_slot = owner_index * CAPACITY + slot_rank
    send_rows = (
        jnp.full((peer_count * CAPACITY,), -1, jnp.int32)
        .at[flat_slot]
        .set(row_index)
        .reshape(peer_count, CAPACITY)
    )
    asked_rows = lax.all_to_all(
        send_rows, ("mode", "group"), split_axis=0, concat_axis=0, tiled=True
    )
    safe_rows = jnp.maximum(asked_rows, 0).reshape(-1)
    final_table = complex_table(final_branch)
    results = jnp.einsum(
        "zlr,zrwk->wlk", stem_rows, final_table, preferred_element_type=jnp.float32
    ).astype(jnp.bfloat16)
    picked = jnp.take(results, safe_rows, axis=1).reshape(2, peer_count, CAPACITY, results.shape[2])
    returned = lax.all_to_all(picked, ("mode", "group"), split_axis=1, concat_axis=1, tiled=True)
    amplitudes = jnp.take(
        returned.reshape(2, peer_count * CAPACITY, results.shape[2]), flat_slot, axis=1
    )
    return amplitudes[:, None]


def per_device(mode_size, group_size, *arguments):
    stem_slice, _, row, mode, final, _, _, requests = arguments
    peers = mode_size * group_size
    row_count, width = stem_slice.shape[2:]
    padded = -(-requests.shape[1] // 16) * 16
    fits = (
        peers == TILE
        and padded <= width
        and row.shape[1] == width
        and mode.shape[1] % (16 * peers) == 0
        and row_count % (ROWS_STEP * width) == 0
        and 2 * peers * padded * final.shape[2] < stem_slice.size
    )
    if fits:
        return fused(mode_size, group_size, padded, arguments)
    return swapped(*arguments)


def solution(mesh):
    return jax.shard_map(
        functools.partial(per_device, mesh.shape["mode"], mesh.shape["group"]),
        mesh=mesh,
        in_specs=(
            P(None, ("cuts", "batch"), ("mode", "group"), None),
            P(),
            P(),
            P(),
            P(),
            P(),
            P(),
            P("batch", ("mode", "group")),
        ),
        out_specs=P(None, ("cuts", "batch"), ("mode", "group"), None),
        check_vma=False,
    )
```

```python
import functools

import jax
import jax.numpy as jnp
from jax import lax
from jax.experimental import pallas as pl
from jax.experimental.pallas import tpu as pltpu
from jax.sharding import PartitionSpec as P

CAPACITY = 8
TILE = 8
ROWS_STEP = 2

F32 = jnp.float32
BF16 = jnp.bfloat16


def dot(left, right):
    return jnp.dot(left, right, preferred_element_type=F32)


def dot_t(left, right):
    return lax.dot_general(left, right, (((1,), (1,)), ((), ())), preferred_element_type=F32)


def iota(shape, dim):
    return lax.broadcasted_iota(jnp.int32, shape, dim)


def complex_rows(real, imag, axis):
    return jnp.concatenate([real, -imag], axis), jnp.concatenate([imag, real], axis)


def fused_kernel(
    mode_size,
    group_size,
    stem_hbm,
    column_hbm,
    row_hbm,
    mode_hbm,
    final_hbm,
    row_labels_hbm,
    mode_labels_hbm,
    requests_hbm,
    out_ref,
    stem,
    column,
    row,
    mode,
    final,
    row_labels,
    mode_labels,
    wanted,
    asked,
    spread,
    picked,
    coeffs,
    partial,
    outgoing,
    incoming,
    load_sem,
    stem_sem,
    ask_send,
    ask_recv,
    give_send,
    give_recv,
):
    peers = mode_size * group_size
    row_count, width = stem.shape[1], stem.shape[2]
    row_order = row.shape[1]
    order = mode.shape[1]
    sub = order // peers
    heads = row_order // sub
    groups = row_count // row_order
    length = final.shape[1]
    fold = length // width
    out_width = final.shape[2]
    count = wanted.shape[1]
    padded = outgoing.shape[1]
    total = peers * padded
    blocks = row_count // sub
    row_blocks = order // fold
    terms = 2 * sub
    span = terms * TILE

    mode_index = lax.axis_index("mode")
    group_index = lax.axis_index("group")
    me = mode_index * group_size + group_index

    def device(offset):
        peer = lax.rem(me + offset, peers)
        return {"mode": peer // group_size, "group": lax.rem(peer, group_size)}

    barrier = pltpu.get_barrier_semaphore()
    for offset in range(1, peers):
        pl.semaphore_signal(
            barrier, inc=1, device_id=device(offset), device_id_type=pl.DeviceIdType.MESH
        )

    small = [
        pltpu.make_async_copy(source, target, load_sem.at[index])
        for index, (source, target) in enumerate(
            (
                (requests_hbm, wanted),
                (column_hbm, column),
                (row_hbm, row),
                (row_labels_hbm, row_labels),
                (mode_hbm, mode),
                (mode_labels_hbm, mode_labels),
                (final_hbm, final),
            )
        )
    ]
    step_rows = ROWS_STEP * row_order
    stem_loads = [
        pltpu.make_async_copy(
            stem_hbm.at[:, 0, pl.ds(step * step_rows, step_rows), :],
            stem.at[:, pl.ds(step * step_rows, step_rows), :],
            stem_sem.at[step],
        )
        for step in range(groups // ROWS_STEP)
    ]
    for load in small[:4] + stem_loads + small[4:]:
        load.start()

    small[0].wait()
    asked[0:1, :] = jnp.zeros((1, width), jnp.int32)
    asked[0:1, 0:count] = wanted[...]

    for load in small[1:4]:
        load.wait()
    column_real, column_imag = complex_rows(column[0], column[1], 0)
    column_table = jnp.concatenate([column_real, column_imag], 1)
    chosen = (iota((row_order, row_order), 0) == row_labels[...]).astype(BF16)
    order_out = iota((row_order, row_order), 0)
    order_in = iota((row_order, row_order), 1)
    swap_rows = (
        order_in == lax.rem(order_out, heads) * sub + lax.div(order_out, heads)
    ).astype(BF16)
    row_real = dot_t(swap_rows, dot(chosen, row[0]).astype(BF16)).astype(BF16)
    row_imag = dot_t(swap_rows, dot(chosen, row[1]).astype(BF16)).astype(BF16)
    row_table = jnp.concatenate(complex_rows(row_real, row_imag, 1), 0)

    pl.semaphore_wait(barrier, peers - 1)
    asks = [
        pltpu.make_async_remote_copy(
            src_ref=asked.at[pl.ds(0, 1), :],
            dst_ref=asked.at[pl.ds(offset, 1), :],
            send_sem=ask_send.at[offset],
            recv_sem=ask_recv.at[offset],
            device_id=device(offset),
            device_id_type=pl.DeviceIdType.MESH,
        )
        for offset in range(1, peers)
    ]
    for ask in asks:
        ask.start()

    for step in range(groups // ROWS_STEP):
        stem_loads[step].wait()
        rows = pl.ds(step * step_rows, step_rows)
        operand = jnp.concatenate([stem[0, rows, :], stem[1, rows, :]], 1)
        mixed = dot(operand, column_table).astype(BF16)
        pieces = []
        for index in range(ROWS_STEP):
            piece = mixed[index * row_order : (index + 1) * row_order]
            pieces.append(jnp.concatenate([piece[:, :width], piece[:, width:]], 0))
        result = dot(row_table, jnp.concatenate(pieces, 1))
        for index in range(ROWS_STEP):
            first = (step * ROWS_STEP + index) * heads
            spread[:, first : first + heads, :] = result[
                :, index * width : (index + 1) * width
            ].reshape(terms, heads, width)

    for load in small[4:6]:
        load.wait()
    own = (iota((sub, order), 0) + me * sub == mode_labels[...]).astype(BF16)
    mode_real, mode_imag = dot(own, mode[0]), dot(own, mode[1])
    repeat = (lax.div(iota((span, terms), 0), TILE) == iota((span, terms), 1)).astype(BF16)
    mode_table = jnp.concatenate(
        [dot(repeat, half.astype(BF16)) for half in complex_rows(mode_real, mode_imag, 0)], 0
    ).astype(BF16)

    for ask in asks:
        ask.wait()
    ids = asked[...]
    block_ids = jnp.transpose(lax.div(ids, row_blocks).astype(F32))
    order_ids = jnp.transpose((lax.rem(ids, row_blocks) * fold).astype(F32))

    def column_of(values, lanes):
        return jnp.concatenate(
            [
                jnp.broadcast_to(values[:padded, slot : slot + 1], (padded, lanes))
                for slot in range(peers)
            ],
            0,
        )

    lane = iota((total, blocks), 1).astype(F32)
    pick = (column_of(block_ids, blocks) == lane).astype(BF16)
    for term in range(0, terms, 2):
        pair = jnp.concatenate([spread[term], spread[term + 1]], 1).astype(BF16)
        found = dot(pick, pair)
        picked[term] = found[:, :width]
        picked[term + 1] = found[:, width:]

    order_column = column_of(order_ids, order)
    lane = iota((total, order), 1).astype(F32)
    same = lax.rem(iota((total, 2 * span), 0), TILE) == lax.rem(iota((total, 2 * span), 1), TILE)
    for index in range(fold):
        at = (order_column + float(index) == lane).astype(BF16)
        values = jnp.where(same, dot_t(at, mode_table), 0.0)
        coeffs[index] = values[:, :span]
        coeffs[fold + index] = values[:, span:]

    for tile in range(total // TILE):
        rows = pl.ds(tile * TILE, TILE)
        left = coeffs[:, rows, :].reshape(2 * fold * TILE, span).astype(BF16)
        right = picked[:, rows, :].reshape(span, width).astype(BF16)
        partial[:, rows, :] = dot(left, right).reshape(2 * fold, TILE, width)

    small[6].wait()
    halves = []
    for half in range(2):
        halves.append(
            jnp.concatenate(
                [partial[half * fold + index].astype(BF16) for index in range(fold)], 1
            )
        )
    products = dot(halves[0], jnp.concatenate([final[0], final[1]], 1)) + dot(
        halves[1], jnp.concatenate([-final[1], final[0]], 1)
    )
    outgoing[...] = products.reshape(peers, padded, 2 * out_width).astype(BF16)

    gives = [
        pltpu.make_async_remote_copy(
            src_ref=outgoing.at[offset],
            dst_ref=incoming.at[offset],
            send_sem=give_send.at[offset],
            recv_sem=give_recv.at[offset],
            device_id=device(peers - offset),
            device_id_type=pl.DeviceIdType.MESH,
        )
        for offset in range(1, peers)
    ]
    for give in gives:
        give.start()
    answer = products[:padded]
    for offset, give in enumerate(gives, 1):
        give.wait_recv()
        answer = answer + incoming[offset].astype(F32)
    answer = answer.astype(out_ref.dtype)
    out_ref[0, 0] = answer[:count, :out_width]
    out_ref[1, 0] = answer[:count, out_width:]
    for give in gives:
        give.wait_send()


def fused(mode_size, group_size, padded, arguments):
    stem_slice, column, row, mode, final, row_labels, mode_labels, requests = arguments
    peers = mode_size * group_size
    row_count, width = stem_slice.shape[2:]
    order = mode.shape[1]
    sub = order // peers
    fold = final.shape[1] // width
    out_width = final.shape[2]
    count = requests.shape[1]
    total = peers * padded
    terms = 2 * sub
    span = terms * TILE
    steps = row_count // row.shape[1] // ROWS_STEP
    row_labels = row_labels.reshape(1, -1)
    mode_labels = mode_labels.reshape(1, -1)
    dma = pltpu.SemaphoreType.DMA
    return pl.pallas_call(
        functools.partial(fused_kernel, mode_size, group_size),
        out_shape=jax.ShapeDtypeStruct((2, 1, count, out_width), BF16),
        in_specs=[pl.BlockSpec(memory_space=pltpu.HBM)] * 8,
        out_specs=pl.BlockSpec(memory_space=pltpu.VMEM),
        scratch_shapes=[
            pltpu.VMEM((2, row_count, width), BF16),
            pltpu.VMEM(column.shape, BF16),
            pltpu.VMEM(row.shape, BF16),
            pltpu.VMEM(mode.shape, BF16),
            pltpu.VMEM(final.shape, BF16),
            pltpu.VMEM(row_labels.shape, jnp.int32),
            pltpu.VMEM(mode_labels.shape, jnp.int32),
            pltpu.VMEM(requests.shape, jnp.int32),
            pltpu.VMEM((peers, width), jnp.int32),
            pltpu.VMEM((terms, row_count // sub, width), F32),
            pltpu.VMEM((terms, total, width), F32),
            pltpu.VMEM((2 * fold, total, span), F32),
            pltpu.VMEM((2 * fold, total, width), F32),
            pltpu.VMEM((peers, padded, 2 * out_width), BF16),
            pltpu.VMEM((peers, padded, 2 * out_width), BF16),
            dma((7,)),
            dma((steps,)),
            dma((peers,)),
            dma((peers,)),
            dma((peers,)),
            dma((peers,)),
        ],
        compiler_params=pltpu.CompilerParams(
            collective_id=0, has_side_effects=True, vmem_limit_bytes=60 * 1024 * 1024
        ),
    )(stem_slice, column, row, mode, final, row_labels, mode_labels, requests)


def complex_table(weight):
    real_part = weight[0]
    imag_part = weight[1]
    return jnp.stack([jnp.stack([real_part, imag_part], 1), jnp.stack([-imag_part, real_part], 1)])


def relabel(weight, labels):
    label_count = labels.shape[0]
    onehot = (labels[:, None] == jnp.arange(label_count, dtype=jnp.int32)[None, :]).astype(
        jnp.float32
    )
    relabelled = jnp.einsum(
        "ji,zjn->zin", onehot, weight.astype(jnp.float32), precision=lax.Precision.HIGHEST
    )
    return complex_table(relabelled.astype(jnp.bfloat16))


def swapped(
    stem_slice,
    column_branch,
    row_branch,
    mode_branch,
    final_branch,
    row_labels,
    mode_labels,
    requests,
):
    local_block = stem_slice[:, 0]
    row_count = local_block.shape[1]
    col_width = local_block.shape[2]
    first_mixed = jnp.einsum(
        "zlc,zcwk->wlk",
        local_block,
        complex_table(column_branch),
        preferred_element_type=jnp.float32,
    ).astype(jnp.bfloat16)
    grouped = first_mixed.reshape(2, row_count // col_width, col_width, col_width)
    second = jnp.einsum(
        "zgjc,zjwk->wgkc",
        grouped,
        relabel(row_branch, row_labels),
        preferred_element_type=jnp.float32,
    ).astype(jnp.bfloat16)
    peer_count = lax.axis_size(("mode", "group"))
    order_size = mode_branch.shape[1]
    sub_rows = order_size // peer_count
    blocks = row_count // order_size
    mode_table = relabel(mode_branch, mode_labels).reshape(2, peer_count, sub_rows, 2, order_size)
    shaped = second.reshape(2, peer_count, blocks, sub_rows, col_width)
    mode_mixed = jnp.einsum(
        "zqhsc,zqswk->whkc",
        lax.all_to_all(shaped, ("mode", "group"), split_axis=1, concat_axis=1, tiled=True),
        mode_table,
        preferred_element_type=jnp.float32,
    ).astype(jnp.bfloat16)
    stem_rows = mode_mixed.reshape(2, row_count // 8, 8 * col_width)
    row_total = stem_rows.shape[1]
    wanted = requests[0]
    owner_index = wanted // row_total
    row_index = wanted - owner_index * row_total
    peer_ids = jnp.arange(peer_count, dtype=jnp.int32)
    onehot = (owner_index[:, None] == peer_ids[None, :]).astype(jnp.int32)
    slot_rank = jnp.sum((jnp.cumsum(onehot, axis=0) - onehot) * onehot, axis=1)
    flat_slot = owner_index * CAPACITY + slot_rank
    send_rows = (
        jnp.full((peer_count * CAPACITY,), -1, jnp.int32)
        .at[flat_slot]
        .set(row_index)
        .reshape(peer_count, CAPACITY)
    )
    asked_rows = lax.all_to_all(
        send_rows, ("mode", "group"), split_axis=0, concat_axis=0, tiled=True
    )
    safe_rows = jnp.maximum(asked_rows, 0).reshape(-1)
    final_table = complex_table(final_branch)
    results = jnp.einsum(
        "zlr,zrwk->wlk", stem_rows, final_table, preferred_element_type=jnp.float32
    ).astype(jnp.bfloat16)
    picked = jnp.take(results, safe_rows, axis=1).reshape(2, peer_count, CAPACITY, results.shape[2])
    returned = lax.all_to_all(picked, ("mode", "group"), split_axis=1, concat_axis=1, tiled=True)
    amplitudes = jnp.take(
        returned.reshape(2, peer_count * CAPACITY, results.shape[2]), flat_slot, axis=1
    )
    return amplitudes[:, None]


def per_device(mode_size, group_size, *arguments):
    stem_slice, _, row, mode, final, _, _, requests = arguments
    peers = mode_size * group_size
    row_count, width = stem_slice.shape[2:]
    padded = -(-requests.shape[1] // 16) * 16
    fits = (
        peers == TILE
        and padded <= width
        and row.shape[1] == width
        and mode.shape[1] % (16 * peers) == 0
        and row_count % (ROWS_STEP * width) == 0
        and 2 * peers * padded * final.shape[2] < stem_slice.size
    )
    if fits:
        return fused(mode_size, group_size, padded, arguments)
    return swapped(*arguments)


def solution(mesh):
    return jax.shard_map(
        functools.partial(per_device, mesh.shape["mode"], mesh.shape["group"]),
        mesh=mesh,
        in_specs=(
            P(None, ("cuts", "batch"), ("mode", "group"), None),
            P(),
            P(),
            P(),
            P(),
            P(),
            P(),
            P("batch", ("mode", "group")),
        ),
        out_specs=P(None, ("cuts", "batch"), ("mode", "group"), None),
        check_vma=False,
    )
```

```python
import functools

import jax
import jax.numpy as jnp
from jax import lax
from jax.experimental import pallas as pl
from jax.experimental.pallas import tpu as pltpu
from jax.sharding import PartitionSpec as P

CAPACITY = 8
TILE = 8
ROWS_STEP = 2

F32 = jnp.float32
BF16 = jnp.bfloat16


def dot(left, right):
    return jnp.dot(left, right, preferred_element_type=F32)


def dot_t(left, right):
    return lax.dot_general(left, right, (((1,), (1,)), ((), ())), preferred_element_type=F32)


def iota(shape, dim):
    return lax.broadcasted_iota(jnp.int32, shape, dim)


def complex_rows(real, imag, axis):
    return jnp.concatenate([real, -imag], axis), jnp.concatenate([imag, real], axis)


def fused_kernel(
    mode_size,
    group_size,
    stem_hbm,
    column_hbm,
    row_hbm,
    mode_hbm,
    final_hbm,
    row_labels_hbm,
    mode_labels_hbm,
    requests_hbm,
    out_ref,
    stem,
    column,
    row,
    mode,
    final,
    row_labels,
    mode_labels,
    wanted,
    asked,
    spread,
    picked,
    coeffs,
    partial,
    outgoing,
    incoming,
    load_sem,
    stem_sem,
    ask_send,
    ask_recv,
    give_send,
    give_recv,
):
    peers = mode_size * group_size
    row_count, width = stem.shape[1], stem.shape[2]
    row_order = row.shape[1]
    order = mode.shape[1]
    sub = order // peers
    heads = row_order // sub
    groups = row_count // row_order
    length = final.shape[1]
    fold = length // width
    out_width = final.shape[2]
    count = wanted.shape[1]
    padded = outgoing.shape[1]
    total = peers * padded
    blocks = row_count // sub
    row_blocks = order // fold
    terms = 2 * sub
    span = terms * TILE
    tiles = total // TILE

    mode_index = lax.axis_index("mode")
    group_index = lax.axis_index("group")
    me = mode_index * group_size + group_index

    def device(offset):
        peer = lax.rem(me + offset, peers)
        return {"mode": peer // group_size, "group": lax.rem(peer, group_size)}

    barrier = pltpu.get_barrier_semaphore()
    for offset in range(1, peers):
        pl.semaphore_signal(
            barrier, inc=1, device_id=device(offset), device_id_type=pl.DeviceIdType.MESH
        )

    small = [
        pltpu.make_async_copy(source, target, load_sem.at[index])
        for index, (source, target) in enumerate(
            (
                (requests_hbm, wanted),
                (column_hbm, column),
                (row_hbm, row),
                (row_labels_hbm, row_labels),
                (mode_hbm, mode),
                (mode_labels_hbm, mode_labels),
                (final_hbm, final),
            )
        )
    ]
    step_rows = ROWS_STEP * row_order
    stem_loads = [
        pltpu.make_async_copy(
            stem_hbm.at[:, 0, pl.ds(step * step_rows, step_rows), :],
            stem.at[:, pl.ds(step * step_rows, step_rows), :],
            stem_sem.at[step],
        )
        for step in range(groups // ROWS_STEP)
    ]
    for load in small[:4] + stem_loads + small[4:]:
        load.start()

    small[0].wait()
    asked[0:1, :] = jnp.zeros((1, width), jnp.int32)
    asked[0:1, 0:count] = wanted[...]
    for load in small[1:4] + stem_loads:
        load.wait()

    column_real, column_imag = complex_rows(column[0], column[1], 0)
    column_table = jnp.concatenate([column_real, column_imag], 1)
    chosen = (iota((row_order, row_order), 0) == row_labels[...]).astype(BF16)
    cube = (sub, heads, row_order)
    swap_rows = (
        (iota(cube, 1) * sub + iota(cube, 0) == iota(cube, 2))
        .astype(F32)
        .reshape(row_order, row_order)
        .astype(BF16)
    )
    row_real = dot_t(swap_rows, dot(chosen, row[0]).astype(BF16)).astype(BF16)
    row_imag = dot_t(swap_rows, dot(chosen, row[1]).astype(BF16)).astype(BF16)
    row_table = jnp.concatenate(complex_rows(row_real, row_imag, 1), 0)

    def mix(step):
        rows = pl.ds(step * step_rows, step_rows)
        operand = jnp.concatenate([stem[0, rows, :], stem[1, rows, :]], 1)
        mixed = dot(operand, column_table).astype(BF16)
        pieces = []
        for index in range(ROWS_STEP):
            piece = mixed[index * row_order : (index + 1) * row_order]
            pieces.append(jnp.concatenate([piece[:, :width], piece[:, width:]], 0))
        result = dot(row_table, jnp.concatenate(pieces, 1))
        result = [
            result[:, index * width : (index + 1) * width].reshape(terms, heads, width)
            for index in range(ROWS_STEP)
        ]
        first = step * ROWS_STEP * heads
        spread[:, first : first + ROWS_STEP * heads, :] = jnp.concatenate(result, 1).astype(BF16)

    steps = groups // ROWS_STEP
    for step in range(steps // 2):
        mix(step)

    pl.semaphore_wait(barrier, peers - 1)
    asks = [
        pltpu.make_async_remote_copy(
            src_ref=asked.at[pl.ds(0, 1), :],
            dst_ref=asked.at[pl.ds(offset, 1), :],
            send_sem=ask_send.at[offset],
            recv_sem=ask_recv.at[offset],
            device_id=device(offset),
            device_id_type=pl.DeviceIdType.MESH,
        )
        for offset in range(1, peers)
    ]
    for ask in asks:
        ask.start()
    for load in small[4:]:
        load.wait()

    for step in range(steps // 2, steps):
        mix(step)

    own = (iota((sub, order), 0) + me * sub == mode_labels[...]).astype(BF16)
    mode_real, mode_imag = dot(own, mode[0]), dot(own, mode[1])
    cube = (terms, TILE, terms)
    repeat = (iota(cube, 0) == iota(cube, 2)).astype(F32).reshape(span, terms).astype(BF16)
    mode_table = jnp.concatenate(
        [dot(repeat, half.astype(BF16)) for half in complex_rows(mode_real, mode_imag, 0)], 0
    ).astype(BF16)

    for ask in asks:
        ask.wait_recv()
    ids = asked[...]
    block_ids = jnp.transpose(lax.div(ids, row_blocks).astype(F32))
    order_ids = jnp.transpose((lax.rem(ids, row_blocks) * fold).astype(F32))

    def column_of(values, lanes):
        return jnp.concatenate(
            [
                jnp.broadcast_to(values[:padded, slot : slot + 1], (padded, lanes))
                for slot in range(peers)
            ],
            0,
        )

    def paired(first, second):
        lanes = first.shape[1]
        both = [part.reshape(tiles, TILE, lanes) for part in (first, second)]
        return jnp.concatenate(both, 1).astype(BF16)

    lane = iota((total, blocks), 1).astype(F32)
    pick = (column_of(block_ids, blocks) == lane).astype(BF16)
    for term in range(0, terms, 2):
        found = dot(pick, jnp.concatenate([spread[term], spread[term + 1]], 1))
        picked[:, term * TILE : (term + 2) * TILE, :] = paired(found[:, :width], found[:, width:])

    order_column = column_of(order_ids, order)
    lane = iota((total, order), 1).astype(F32)
    same = (iota((TILE, 2 * span), 1) & (TILE - 1)) == iota((TILE, 2 * span), 0)
    same = jnp.broadcast_to(same[None], (tiles, TILE, 2 * span)).reshape(total, 2 * span)

    def coefficients(index):
        at = (order_column + float(index) == lane).astype(BF16)
        return jnp.where(same, dot_t(at, mode_table), 0.0)

    for index in range(0, fold, 2):
        first, second = coefficients(index), coefficients(index + 1)
        for half in range(2):
            rows = (half * fold + index) * TILE
            lanes = slice(half * span, (half + 1) * span)
            coeffs[:, rows : rows + 2 * TILE, :] = paired(first[:, lanes], second[:, lanes])

    final_real = jnp.concatenate([final[0], final[1]], 1)
    final_imag = jnp.concatenate([-final[1], final[0]], 1)

    def products(first_slot, last_slot):
        first, last = first_slot * padded, last_slot * padded
        for row_start in range(first, last, 2 * TILE):
            tile = row_start // TILE
            both = [
                dot(coeffs[tile + index], picked[tile + index]).reshape(2 * fold, TILE, width)
                for index in range(2)
            ]
            partial[:, row_start : row_start + 2 * TILE, :] = jnp.concatenate(both, 1).astype(BF16)
        rows = slice(first, last)
        real = jnp.concatenate([partial[index, rows] for index in range(fold)], 1)
        imag = jnp.concatenate([partial[fold + index, rows] for index in range(fold)], 1)
        return dot(real, final_real) + dot(imag, final_imag)

    gives = [
        pltpu.make_async_remote_copy(
            src_ref=outgoing.at[offset],
            dst_ref=incoming.at[offset],
            send_sem=give_send.at[offset],
            recv_sem=give_recv.at[offset],
            device_id=device(peers - offset),
            device_id_type=pl.DeviceIdType.MESH,
        )
        for offset in range(1, peers)
    ]
    middle = peers // 2
    result = products(middle, peers)
    outgoing[middle:] = result.reshape(peers - middle, padded, 2 * out_width).astype(BF16)
    for give in gives[middle - 1 :]:
        give.start()
    result = products(0, middle)
    outgoing[:middle] = result.reshape(middle, padded, 2 * out_width).astype(BF16)
    for give in gives[: middle - 1]:
        give.start()
    answer = result[:padded]
    for offset in list(range(middle, peers)) + list(range(1, middle)):
        gives[offset - 1].wait_recv()
        answer = answer + incoming[offset].astype(F32)
    answer = answer.astype(out_ref.dtype)
    out_ref[0, 0] = answer[:count, :out_width]
    out_ref[1, 0] = answer[:count, out_width:]
    for copy in asks + gives:
        copy.wait_send()


def fused(mode_size, group_size, padded, arguments):
    stem_slice, column, row, mode, final, row_labels, mode_labels, requests = arguments
    peers = mode_size * group_size
    row_count, width = stem_slice.shape[2:]
    order = mode.shape[1]
    sub = order // peers
    fold = final.shape[1] // width
    out_width = final.shape[2]
    count = requests.shape[1]
    total = peers * padded
    terms = 2 * sub
    span = terms * TILE
    steps = row_count // row.shape[1] // ROWS_STEP
    row_labels = row_labels.reshape(1, -1)
    mode_labels = mode_labels.reshape(1, -1)
    dma = pltpu.SemaphoreType.DMA
    return pl.pallas_call(
        functools.partial(fused_kernel, mode_size, group_size),
        out_shape=jax.ShapeDtypeStruct((2, 1, count, out_width), BF16),
        in_specs=[pl.BlockSpec(memory_space=pltpu.HBM)] * 8,
        out_specs=pl.BlockSpec(memory_space=pltpu.VMEM),
        scratch_shapes=[
            pltpu.VMEM((2, row_count, width), BF16),
            pltpu.VMEM(column.shape, BF16),
            pltpu.VMEM(row.shape, BF16),
            pltpu.VMEM(mode.shape, BF16),
            pltpu.VMEM(final.shape, BF16),
            pltpu.VMEM(row_labels.shape, jnp.int32),
            pltpu.VMEM(mode_labels.shape, jnp.int32),
            pltpu.VMEM(requests.shape, jnp.int32),
            pltpu.VMEM((peers, width), jnp.int32),
            pltpu.VMEM((terms, row_count // sub, width), BF16),
            pltpu.VMEM((total // TILE, span, width), BF16),
            pltpu.VMEM((total // TILE, 2 * fold * TILE, span), BF16),
            pltpu.VMEM((2 * fold, total, width), BF16),
            pltpu.VMEM((peers, padded, 2 * out_width), BF16),
            pltpu.VMEM((peers, padded, 2 * out_width), BF16),
            dma((7,)),
            dma((steps,)),
            dma((peers,)),
            dma((peers,)),
            dma((peers,)),
            dma((peers,)),
        ],
        compiler_params=pltpu.CompilerParams(
            collective_id=0, has_side_effects=True, vmem_limit_bytes=60 * 1024 * 1024
        ),
    )(stem_slice, column, row, mode, final, row_labels, mode_labels, requests)


def complex_table(weight):
    real_part = weight[0]
    imag_part = weight[1]
    return jnp.stack([jnp.stack([real_part, imag_part], 1), jnp.stack([-imag_part, real_part], 1)])


def relabel(weight, labels):
    label_count = labels.shape[0]
    onehot = (labels[:, None] == jnp.arange(label_count, dtype=jnp.int32)[None, :]).astype(
        jnp.float32
    )
    relabelled = jnp.einsum(
        "ji,zjn->zin", onehot, weight.astype(jnp.float32), precision=lax.Precision.HIGHEST
    )
    return complex_table(relabelled.astype(jnp.bfloat16))


def swapped(
    stem_slice,
    column_branch,
    row_branch,
    mode_branch,
    final_branch,
    row_labels,
    mode_labels,
    requests,
):
    local_block = stem_slice[:, 0]
    row_count = local_block.shape[1]
    col_width = local_block.shape[2]
    first_mixed = jnp.einsum(
        "zlc,zcwk->wlk",
        local_block,
        complex_table(column_branch),
        preferred_element_type=jnp.float32,
    ).astype(jnp.bfloat16)
    grouped = first_mixed.reshape(2, row_count // col_width, col_width, col_width)
    second = jnp.einsum(
        "zgjc,zjwk->wgkc",
        grouped,
        relabel(row_branch, row_labels),
        preferred_element_type=jnp.float32,
    ).astype(jnp.bfloat16)
    peer_count = lax.axis_size(("mode", "group"))
    order_size = mode_branch.shape[1]
    sub_rows = order_size // peer_count
    blocks = row_count // order_size
    mode_table = relabel(mode_branch, mode_labels).reshape(2, peer_count, sub_rows, 2, order_size)
    shaped = second.reshape(2, peer_count, blocks, sub_rows, col_width)
    mode_mixed = jnp.einsum(
        "zqhsc,zqswk->whkc",
        lax.all_to_all(shaped, ("mode", "group"), split_axis=1, concat_axis=1, tiled=True),
        mode_table,
        preferred_element_type=jnp.float32,
    ).astype(jnp.bfloat16)
    stem_rows = mode_mixed.reshape(2, row_count // 8, 8 * col_width)
    row_total = stem_rows.shape[1]
    wanted = requests[0]
    owner_index = wanted // row_total
    row_index = wanted - owner_index * row_total
    peer_ids = jnp.arange(peer_count, dtype=jnp.int32)
    onehot = (owner_index[:, None] == peer_ids[None, :]).astype(jnp.int32)
    slot_rank = jnp.sum((jnp.cumsum(onehot, axis=0) - onehot) * onehot, axis=1)
    flat_slot = owner_index * CAPACITY + slot_rank
    send_rows = (
        jnp.full((peer_count * CAPACITY,), -1, jnp.int32)
        .at[flat_slot]
        .set(row_index)
        .reshape(peer_count, CAPACITY)
    )
    asked_rows = lax.all_to_all(
        send_rows, ("mode", "group"), split_axis=0, concat_axis=0, tiled=True
    )
    safe_rows = jnp.maximum(asked_rows, 0).reshape(-1)
    final_table = complex_table(final_branch)
    results = jnp.einsum(
        "zlr,zrwk->wlk", stem_rows, final_table, preferred_element_type=jnp.float32
    ).astype(jnp.bfloat16)
    picked = jnp.take(results, safe_rows, axis=1).reshape(2, peer_count, CAPACITY, results.shape[2])
    returned = lax.all_to_all(picked, ("mode", "group"), split_axis=1, concat_axis=1, tiled=True)
    amplitudes = jnp.take(
        returned.reshape(2, peer_count * CAPACITY, results.shape[2]), flat_slot, axis=1
    )
    return amplitudes[:, None]


def per_device(mode_size, group_size, *arguments):
    stem_slice, _, row, mode, final, _, _, requests = arguments
    peers = mode_size * group_size
    row_count, width = stem_slice.shape[2:]
    padded = -(-requests.shape[1] // 16) * 16
    fits = (
        peers == TILE
        and padded <= width
        and row.shape[1] == width
        and mode.shape[1] % (16 * peers) == 0
        and row_count % (ROWS_STEP * width) == 0
        and 2 * peers * padded * final.shape[2] < stem_slice.size
    )
    if fits:
        return fused(mode_size, group_size, padded, arguments)
    return swapped(*arguments)


def solution(mesh):
    return jax.shard_map(
        functools.partial(per_device, mesh.shape["mode"], mesh.shape["group"]),
        mesh=mesh,
        in_specs=(
            P(None, ("cuts", "batch"), ("mode", "group"), None),
            P(),
            P(),
            P(),
            P(),
            P(),
            P(),
            P("batch", ("mode", "group")),
        ),
        out_specs=P(None, ("cuts", "batch"), ("mode", "group"), None),
        check_vma=False,
    )
```

```python
import functools

import jax
import jax.numpy as jnp
from jax import lax
from jax.experimental import pallas as pl
from jax.experimental.pallas import tpu as pltpu
from jax.sharding import PartitionSpec as P

CAPACITY = 8
TILE = 8
ROWS_STEP = 2

F32 = jnp.float32
BF16 = jnp.bfloat16


def dot(left, right):
    return jnp.dot(left, right, preferred_element_type=F32)


def dot_t(left, right):
    return lax.dot_general(left, right, (((1,), (1,)), ((), ())), preferred_element_type=F32)


def iota(shape, dim):
    return lax.broadcasted_iota(jnp.int32, shape, dim)


def loop(start, stop, body, unroll=2):
    def run(trip, carry):
        for index in range(unroll):
            body(start + trip * unroll + index)
        return carry

    trips = (stop - start) // unroll
    lax.fori_loop(0, trips, run, 0)
    for step in range(start + trips * unroll, stop):
        body(step)


def complex_rows(real, imag, axis):
    return jnp.concatenate([real, -imag], axis), jnp.concatenate([imag, real], axis)


def fused_kernel(
    mode_size,
    group_size,
    stem_hbm,
    column_hbm,
    row_hbm,
    mode_hbm,
    final_hbm,
    row_labels_hbm,
    mode_labels_hbm,
    requests_hbm,
    out_ref,
    stem,
    column,
    row,
    mode,
    final,
    row_labels,
    mode_labels,
    wanted,
    asked,
    spread,
    picked,
    coeffs,
    partial,
    outgoing,
    incoming,
    load_sem,
    stem_sem,
    ask_send,
    ask_recv,
    give_send,
    give_recv,
):
    peers = mode_size * group_size
    row_count, width = stem.shape[1], stem.shape[2]
    row_order = row.shape[1]
    order = mode.shape[1]
    sub = order // peers
    heads = row_order // sub
    groups = row_count // row_order
    length = final.shape[1]
    fold = length // width
    out_width = final.shape[2]
    count = wanted.shape[1]
    padded = outgoing.shape[1]
    total = peers * padded
    blocks = row_count // sub
    row_blocks = order // fold
    terms = 2 * sub
    span = terms * TILE
    tiles = total // TILE

    mode_index = lax.axis_index("mode")
    group_index = lax.axis_index("group")
    me = mode_index * group_size + group_index

    def device(offset):
        peer = lax.rem(me + offset, peers)
        return {"mode": peer // group_size, "group": lax.rem(peer, group_size)}

    barrier = pltpu.get_barrier_semaphore()
    for offset in range(1, peers):
        pl.semaphore_signal(
            barrier, inc=1, device_id=device(offset), device_id_type=pl.DeviceIdType.MESH
        )

    small = [
        pltpu.make_async_copy(source, target, load_sem.at[index])
        for index, (source, target) in enumerate(
            (
                (requests_hbm, wanted),
                (column_hbm, column),
                (row_hbm, row),
                (row_labels_hbm, row_labels),
                (mode_hbm, mode),
                (mode_labels_hbm, mode_labels),
                (final_hbm, final),
            )
        )
    ]
    step_rows = ROWS_STEP * row_order
    stem_loads = [
        pltpu.make_async_copy(
            stem_hbm.at[:, 0, pl.ds(step * step_rows, step_rows), :],
            stem.at[:, pl.ds(step * step_rows, step_rows), :],
            stem_sem.at[step],
        )
        for step in range(groups // ROWS_STEP)
    ]
    for load in small[:4] + stem_loads + small[4:]:
        load.start()

    small[0].wait()
    asked[0:1, :] = jnp.zeros((1, width), jnp.int32)
    asked[0:1, 0:count] = wanted[...]
    for load in small[1:4] + stem_loads:
        load.wait()

    column_real, column_imag = complex_rows(column[0], column[1], 0)
    column_table = jnp.concatenate([column_real, column_imag], 1)
    chosen = (iota((row_order, row_order), 0) == row_labels[...]).astype(BF16)
    cube = (sub, heads, row_order)
    swap_rows = (
        (iota(cube, 1) * sub + iota(cube, 0) == iota(cube, 2))
        .astype(F32)
        .reshape(row_order, row_order)
        .astype(BF16)
    )
    row_real = dot_t(swap_rows, dot(chosen, row[0]).astype(BF16)).astype(BF16)
    row_imag = dot_t(swap_rows, dot(chosen, row[1]).astype(BF16)).astype(BF16)
    row_table = jnp.concatenate(complex_rows(row_real, row_imag, 1), 0)

    def mix(step):
        rows = pl.ds(pl.multiple_of(step * step_rows, step_rows), step_rows)
        operand = jnp.concatenate([stem[0, rows, :], stem[1, rows, :]], 1)
        mixed = dot(operand, column_table).astype(BF16)
        pieces = []
        for index in range(ROWS_STEP):
            piece = mixed[index * row_order : (index + 1) * row_order]
            pieces.append(jnp.concatenate([piece[:, :width], piece[:, width:]], 0))
        result = dot(row_table, jnp.concatenate(pieces, 1))
        result = [
            result[:, index * width : (index + 1) * width].reshape(terms, heads, width)
            for index in range(ROWS_STEP)
        ]
        found = pl.ds(pl.multiple_of(step * ROWS_STEP * heads, 16), ROWS_STEP * heads)
        spread[:, found, :] = jnp.concatenate(result, 1).astype(BF16)

    steps = groups // ROWS_STEP
    loop(0, steps // 2, mix)

    pl.semaphore_wait(barrier, peers - 1)
    asks = [
        pltpu.make_async_remote_copy(
            src_ref=asked.at[pl.ds(0, 1), :],
            dst_ref=asked.at[pl.ds(offset, 1), :],
            send_sem=ask_send.at[offset],
            recv_sem=ask_recv.at[offset],
            device_id=device(offset),
            device_id_type=pl.DeviceIdType.MESH,
        )
        for offset in range(1, peers)
    ]
    for ask in asks:
        ask.start()
    for load in small[4:]:
        load.wait()

    loop(steps // 2, steps, mix)

    own = (iota((sub, order), 0) + me * sub == mode_labels[...]).astype(BF16)
    mode_real, mode_imag = dot(own, mode[0]), dot(own, mode[1])
    cube = (terms, TILE, terms)
    repeat = (iota(cube, 0) == iota(cube, 2)).astype(F32).reshape(span, terms).astype(BF16)
    mode_table = jnp.concatenate(
        [dot(repeat, half.astype(BF16)) for half in complex_rows(mode_real, mode_imag, 0)], 0
    ).astype(BF16)

    for ask in asks:
        ask.wait_recv()
    ids = asked[...]
    block_ids = jnp.transpose(lax.div(ids, row_blocks).astype(F32))
    order_ids = jnp.transpose((lax.rem(ids, row_blocks) * fold).astype(F32))

    def column_of(values, lanes):
        return jnp.concatenate(
            [
                jnp.broadcast_to(values[:padded, slot : slot + 1], (padded, lanes))
                for slot in range(peers)
            ],
            0,
        )

    def paired(first, second):
        lanes = first.shape[1]
        both = [part.reshape(tiles, TILE, lanes) for part in (first, second)]
        return jnp.concatenate(both, 1).astype(BF16)

    lane = iota((total, blocks), 1).astype(F32)
    pick = (column_of(block_ids, blocks) == lane).astype(BF16)

    def pick_pair(pair):
        found = dot(pick, jnp.concatenate([spread[2 * pair], spread[2 * pair + 1]], 1))
        rows = pl.ds(pl.multiple_of(pair * 2 * TILE, 2 * TILE), 2 * TILE)
        picked[:, rows, :] = paired(found[:, :width], found[:, width:])

    loop(0, terms // 2, pick_pair)

    order_column = column_of(order_ids, order).astype(jnp.int32)
    lane = iota((total, order), 1)
    same = (iota((TILE, 2 * span), 1) & (TILE - 1)) == iota((TILE, 2 * span), 0)
    same = jnp.broadcast_to(same[None], (tiles, TILE, 2 * span)).reshape(total, 2 * span)

    def coefficients(index):
        at = (order_column == lane - index).astype(BF16)
        return jnp.where(same, dot_t(at, mode_table), 0.0)

    def coefficient_pair(pair):
        first, second = coefficients(2 * pair), coefficients(2 * pair + 1)
        for half in range(2):
            start = (half * (fold // 2) + pair) * 2 * TILE
            rows = pl.ds(pl.multiple_of(start, 2 * TILE), 2 * TILE)
            lanes = slice(half * span, (half + 1) * span)
            coeffs[:, rows, :] = paired(first[:, lanes], second[:, lanes])

    loop(0, fold // 2, coefficient_pair, 1)

    final_real = jnp.concatenate([final[0], final[1]], 1)
    final_imag = jnp.concatenate([-final[1], final[0]], 1)

    def products(first_slot, last_slot):
        first, last = first_slot * padded, last_slot * padded

        def tile_pair(pair):
            both = [
                dot(coeffs[2 * pair + index], picked[2 * pair + index]).reshape(
                    2 * fold, TILE, width
                )
                for index in range(2)
            ]
            rows = pl.ds(pl.multiple_of(pair * 2 * TILE, 2 * TILE), 2 * TILE)
            partial[:, rows, :] = jnp.concatenate(both, 1).astype(BF16)

        loop(first // (2 * TILE), last // (2 * TILE), tile_pair, 4)
        rows = slice(first, last)
        real = jnp.concatenate([partial[index, rows] for index in range(fold)], 1)
        imag = jnp.concatenate([partial[fold + index, rows] for index in range(fold)], 1)
        return dot(real, final_real) + dot(imag, final_imag)

    gives = [
        pltpu.make_async_remote_copy(
            src_ref=outgoing.at[offset],
            dst_ref=incoming.at[offset],
            send_sem=give_send.at[offset],
            recv_sem=give_recv.at[offset],
            device_id=device(peers - offset),
            device_id_type=pl.DeviceIdType.MESH,
        )
        for offset in range(1, peers)
    ]
    middle = peers // 2
    result = products(middle, peers)
    outgoing[middle:] = result.reshape(peers - middle, padded, 2 * out_width).astype(BF16)
    for give in gives[middle - 1 :]:
        give.start()
    result = products(0, middle)
    outgoing[:middle] = result.reshape(middle, padded, 2 * out_width).astype(BF16)
    for give in gives[: middle - 1]:
        give.start()
    answer = result[:padded]
    for offset in list(range(middle, peers)) + list(range(1, middle)):
        gives[offset - 1].wait_recv()
        answer = answer + incoming[offset].astype(F32)
    answer = answer.astype(out_ref.dtype)
    out_ref[0, 0] = answer[:count, :out_width]
    out_ref[1, 0] = answer[:count, out_width:]
    for copy in asks + gives:
        copy.wait_send()


def fused(mode_size, group_size, padded, arguments):
    stem_slice, column, row, mode, final, row_labels, mode_labels, requests = arguments
    peers = mode_size * group_size
    row_count, width = stem_slice.shape[2:]
    order = mode.shape[1]
    sub = order // peers
    fold = final.shape[1] // width
    out_width = final.shape[2]
    count = requests.shape[1]
    total = peers * padded
    terms = 2 * sub
    span = terms * TILE
    steps = row_count // row.shape[1] // ROWS_STEP
    row_labels = row_labels.reshape(1, -1)
    mode_labels = mode_labels.reshape(1, -1)
    dma = pltpu.SemaphoreType.DMA
    return pl.pallas_call(
        functools.partial(fused_kernel, mode_size, group_size),
        out_shape=pltpu.VMEM((2, 1, count, out_width), BF16),
        in_specs=[pl.BlockSpec(memory_space=pltpu.HBM)] * 8,
        out_specs=pl.BlockSpec(memory_space=pltpu.VMEM),
        scratch_shapes=[
            pltpu.VMEM((2, row_count, width), BF16),
            pltpu.VMEM(column.shape, BF16),
            pltpu.VMEM(row.shape, BF16),
            pltpu.VMEM(mode.shape, BF16),
            pltpu.VMEM(final.shape, BF16),
            pltpu.VMEM(row_labels.shape, jnp.int32),
            pltpu.VMEM(mode_labels.shape, jnp.int32),
            pltpu.VMEM(requests.shape, jnp.int32),
            pltpu.VMEM((peers, width), jnp.int32),
            pltpu.VMEM((terms, row_count // sub, width), BF16),
            pltpu.VMEM((total // TILE, span, width), BF16),
            pltpu.VMEM((total // TILE, 2 * fold * TILE, span), BF16),
            pltpu.VMEM((2 * fold, total, width), BF16),
            pltpu.VMEM((peers, padded, 2 * out_width), BF16),
            pltpu.VMEM((peers, padded, 2 * out_width), BF16),
            dma((7,)),
            dma((steps,)),
            dma((peers,)),
            dma((peers,)),
            dma((peers,)),
            dma((peers,)),
        ],
        compiler_params=pltpu.CompilerParams(
            collective_id=0, has_side_effects=True, vmem_limit_bytes=60 * 1024 * 1024
        ),
    )(stem_slice, column, row, mode, final, row_labels, mode_labels, requests)


def complex_table(weight):
    real_part = weight[0]
    imag_part = weight[1]
    return jnp.stack([jnp.stack([real_part, imag_part], 1), jnp.stack([-imag_part, real_part], 1)])


def relabel(weight, labels):
    label_count = labels.shape[0]
    onehot = (labels[:, None] == jnp.arange(label_count, dtype=jnp.int32)[None, :]).astype(
        jnp.float32
    )
    relabelled = jnp.einsum(
        "ji,zjn->zin", onehot, weight.astype(jnp.float32), precision=lax.Precision.HIGHEST
    )
    return complex_table(relabelled.astype(jnp.bfloat16))


def swapped(
    stem_slice,
    column_branch,
    row_branch,
    mode_branch,
    final_branch,
    row_labels,
    mode_labels,
    requests,
):
    local_block = stem_slice[:, 0]
    row_count = local_block.shape[1]
    col_width = local_block.shape[2]
    first_mixed = jnp.einsum(
        "zlc,zcwk->wlk",
        local_block,
        complex_table(column_branch),
        preferred_element_type=jnp.float32,
    ).astype(jnp.bfloat16)
    grouped = first_mixed.reshape(2, row_count // col_width, col_width, col_width)
    second = jnp.einsum(
        "zgjc,zjwk->wgkc",
        grouped,
        relabel(row_branch, row_labels),
        preferred_element_type=jnp.float32,
    ).astype(jnp.bfloat16)
    peer_count = lax.axis_size(("mode", "group"))
    order_size = mode_branch.shape[1]
    sub_rows = order_size // peer_count
    blocks = row_count // order_size
    mode_table = relabel(mode_branch, mode_labels).reshape(2, peer_count, sub_rows, 2, order_size)
    shaped = second.reshape(2, peer_count, blocks, sub_rows, col_width)
    mode_mixed = jnp.einsum(
        "zqhsc,zqswk->whkc",
        lax.all_to_all(shaped, ("mode", "group"), split_axis=1, concat_axis=1, tiled=True),
        mode_table,
        preferred_element_type=jnp.float32,
    ).astype(jnp.bfloat16)
    stem_rows = mode_mixed.reshape(2, row_count // 8, 8 * col_width)
    row_total = stem_rows.shape[1]
    wanted = requests[0]
    owner_index = wanted // row_total
    row_index = wanted - owner_index * row_total
    peer_ids = jnp.arange(peer_count, dtype=jnp.int32)
    onehot = (owner_index[:, None] == peer_ids[None, :]).astype(jnp.int32)
    slot_rank = jnp.sum((jnp.cumsum(onehot, axis=0) - onehot) * onehot, axis=1)
    flat_slot = owner_index * CAPACITY + slot_rank
    send_rows = (
        jnp.full((peer_count * CAPACITY,), -1, jnp.int32)
        .at[flat_slot]
        .set(row_index)
        .reshape(peer_count, CAPACITY)
    )
    asked_rows = lax.all_to_all(
        send_rows, ("mode", "group"), split_axis=0, concat_axis=0, tiled=True
    )
    safe_rows = jnp.maximum(asked_rows, 0).reshape(-1)
    final_table = complex_table(final_branch)
    results = jnp.einsum(
        "zlr,zrwk->wlk", stem_rows, final_table, preferred_element_type=jnp.float32
    ).astype(jnp.bfloat16)
    picked = jnp.take(results, safe_rows, axis=1).reshape(2, peer_count, CAPACITY, results.shape[2])
    returned = lax.all_to_all(picked, ("mode", "group"), split_axis=1, concat_axis=1, tiled=True)
    amplitudes = jnp.take(
        returned.reshape(2, peer_count * CAPACITY, results.shape[2]), flat_slot, axis=1
    )
    return amplitudes[:, None]


def per_device(mode_size, group_size, *arguments):
    stem_slice, _, row, mode, final, _, _, requests = arguments
    peers = mode_size * group_size
    row_count, width = stem_slice.shape[2:]
    padded = -(-requests.shape[1] // 16) * 16
    fits = (
        peers == TILE
        and padded <= width
        and row.shape[1] == width
        and mode.shape[1] % (16 * peers) == 0
        and row_count % (ROWS_STEP * width) == 0
        and 2 * peers * padded * final.shape[2] < stem_slice.size
    )
    if fits:
        return fused(mode_size, group_size, padded, arguments)
    return swapped(*arguments)


def solution(mesh):
    return jax.shard_map(
        functools.partial(per_device, mesh.shape["mode"], mesh.shape["group"]),
        mesh=mesh,
        in_specs=(
            P(None, ("cuts", "batch"), ("mode", "group"), None),
            P(),
            P(),
            P(),
            P(),
            P(),
            P(),
            P("batch", ("mode", "group")),
        ),
        out_specs=P(None, ("cuts", "batch"), ("mode", "group"), None),
        check_vma=False,
    )
```

```python
import functools

import jax
import jax.numpy as jnp
from jax import lax
from jax.experimental import pallas as pl
from jax.experimental.pallas import tpu as pltpu
from jax.sharding import PartitionSpec as P

CAPACITY = 8
TILE = 8
ROWS_STEP = 2

F32 = jnp.float32
BF16 = jnp.bfloat16


def dot(left, right):
    return jnp.dot(left, right, preferred_element_type=F32)


def dot_t(left, right):
    return lax.dot_general(left, right, (((1,), (1,)), ((), ())), preferred_element_type=F32)


def iota(shape, dim):
    return lax.broadcasted_iota(jnp.int32, shape, dim)


def complex_rows(real, imag, axis):
    return jnp.concatenate([real, -imag], axis), jnp.concatenate([imag, real], axis)


def fused_kernel(
    mode_size,
    group_size,
    stem_hbm,
    column_hbm,
    row_hbm,
    mode_hbm,
    final_hbm,
    row_labels_hbm,
    mode_labels_hbm,
    requests_hbm,
    out_ref,
    stem,
    column,
    row,
    mode,
    final,
    row_labels,
    mode_labels,
    wanted,
    asked,
    spread,
    picked,
    coeffs,
    partial,
    outgoing,
    incoming,
    load_sem,
    stem_sem,
    ask_send,
    ask_recv,
    give_send,
    give_recv,
):
    peers = mode_size * group_size
    row_count, width = stem.shape[1], stem.shape[2]
    row_order = row.shape[1]
    order = mode.shape[1]
    sub = order // peers
    heads = row_order // sub
    groups = row_count // row_order
    length = final.shape[1]
    fold = length // width
    out_width = final.shape[2]
    count = wanted.shape[1]
    padded = outgoing.shape[1]
    total = peers * padded
    blocks = row_count // sub
    row_blocks = order // fold
    terms = 2 * sub
    span = terms * TILE
    tiles = total // TILE

    mode_index = lax.axis_index("mode")
    group_index = lax.axis_index("group")
    me = mode_index * group_size + group_index

    def device(offset):
        peer = lax.rem(me + offset, peers)
        return {"mode": peer // group_size, "group": lax.rem(peer, group_size)}

    barrier = pltpu.get_barrier_semaphore()
    for offset in range(1, peers):
        pl.semaphore_signal(
            barrier, inc=1, device_id=device(offset), device_id_type=pl.DeviceIdType.MESH
        )

    small = [
        pltpu.make_async_copy(source, target, load_sem.at[index])
        for index, (source, target) in enumerate(
            (
                (requests_hbm, wanted),
                (column_hbm, column),
                (row_hbm, row),
                (row_labels_hbm, row_labels),
                (mode_hbm, mode),
                (mode_labels_hbm, mode_labels),
                (final_hbm, final),
            )
        )
    ]
    step_rows = ROWS_STEP * row_order
    stem_loads = [
        pltpu.make_async_copy(
            stem_hbm.at[:, 0, pl.ds(step * step_rows, step_rows), :],
            stem.at[:, pl.ds(step * step_rows, step_rows), :],
            stem_sem.at[step],
        )
        for step in range(groups // ROWS_STEP)
    ]
    for load in small[:4] + stem_loads + small[4:]:
        load.start()

    small[0].wait()
    asked[0:1, :] = jnp.zeros((1, width), jnp.int32)
    asked[0:1, 0:count] = wanted[...]
    for load in small[1:4] + stem_loads:
        load.wait()

    column_real, column_imag = complex_rows(column[0], column[1], 0)
    column_table = jnp.concatenate([column_real, column_imag], 1)
    chosen = (iota((row_order, row_order), 0) == row_labels[...]).astype(BF16)
    cube = (sub, heads, row_order)
    swap_rows = (
        (iota(cube, 1) * sub + iota(cube, 0) == iota(cube, 2))
        .astype(F32)
        .reshape(row_order, row_order)
        .astype(BF16)
    )
    row_real = dot_t(swap_rows, dot(chosen, row[0]).astype(BF16)).astype(BF16)
    row_imag = dot_t(swap_rows, dot(chosen, row[1]).astype(BF16)).astype(BF16)
    row_table = jnp.concatenate(complex_rows(row_real, row_imag, 1), 0)

    def mix(step):
        rows = pl.ds(step * step_rows, step_rows)
        operand = jnp.concatenate([stem[0, rows, :], stem[1, rows, :]], 1)
        mixed = dot(operand, column_table).astype(BF16)
        pieces = []
        for index in range(ROWS_STEP):
            piece = mixed[index * row_order : (index + 1) * row_order]
            pieces.append(jnp.concatenate([piece[:, :width], piece[:, width:]], 0))
        result = dot(row_table, jnp.concatenate(pieces, 1))
        result = [
            result[:, index * width : (index + 1) * width].reshape(terms, heads, width)
            for index in range(ROWS_STEP)
        ]
        first = step * ROWS_STEP * heads
        spread[:, first : first + ROWS_STEP * heads, :] = jnp.concatenate(result, 1).astype(BF16)

    steps = groups // ROWS_STEP
    for step in range(steps // 2):
        mix(step)

    pl.semaphore_wait(barrier, peers - 1)
    asks = [
        pltpu.make_async_remote_copy(
            src_ref=asked.at[pl.ds(0, 1), :],
            dst_ref=asked.at[pl.ds(offset, 1), :],
            send_sem=ask_send.at[offset],
            recv_sem=ask_recv.at[offset],
            device_id=device(offset),
            device_id_type=pl.DeviceIdType.MESH,
        )
        for offset in range(1, peers)
    ]
    for ask in asks:
        ask.start()
    for load in small[4:]:
        load.wait()

    for step in range(steps // 2, steps):
        mix(step)

    own = (iota((sub, order), 0) + me * sub == mode_labels[...]).astype(BF16)
    mode_real, mode_imag = dot(own, mode[0]), dot(own, mode[1])
    cube = (terms, TILE, terms)
    repeat = (iota(cube, 0) == iota(cube, 2)).astype(F32).reshape(span, terms).astype(BF16)
    mode_table = jnp.concatenate(
        [dot(repeat, half.astype(BF16)) for half in complex_rows(mode_real, mode_imag, 0)], 0
    ).astype(BF16)

    for ask in asks:
        ask.wait_recv()
    ids = asked[...]
    block_ids = jnp.transpose(lax.div(ids, row_blocks).astype(F32))
    order_ids = jnp.transpose((lax.rem(ids, row_blocks) * fold).astype(F32))

    def column_of(values, lanes):
        return jnp.concatenate(
            [
                jnp.broadcast_to(values[:padded, slot : slot + 1], (padded, lanes))
                for slot in range(peers)
            ],
            0,
        )

    def paired(first, second):
        lanes = first.shape[1]
        both = [part.reshape(tiles, TILE, lanes) for part in (first, second)]
        return jnp.concatenate(both, 1).astype(BF16)

    lane = iota((total, blocks), 1).astype(F32)
    pick = (column_of(block_ids, blocks) == lane).astype(BF16)
    for term in range(0, terms, 2):
        found = dot(pick, jnp.concatenate([spread[term], spread[term + 1]], 1))
        picked[:, term * TILE : (term + 2) * TILE, :] = paired(found[:, :width], found[:, width:])

    order_column = column_of(order_ids, order)
    lane = iota((total, order), 1).astype(F32)
    same = (iota((TILE, 2 * span), 1) & (TILE - 1)) == iota((TILE, 2 * span), 0)
    same = jnp.broadcast_to(same[None], (tiles, TILE, 2 * span)).reshape(total, 2 * span)

    def coefficients(index):
        at = (order_column + float(index) == lane).astype(BF16)
        return jnp.where(same, dot_t(at, mode_table), 0.0)

    for index in range(0, fold, 2):
        first, second = coefficients(index), coefficients(index + 1)
        for half in range(2):
            rows = (half * fold + index) * TILE
            lanes = slice(half * span, (half + 1) * span)
            coeffs[:, rows : rows + 2 * TILE, :] = paired(first[:, lanes], second[:, lanes])

    final_real = jnp.concatenate([final[0], final[1]], 1)
    final_imag = jnp.concatenate([-final[1], final[0]], 1)

    def products(first_slot, last_slot):
        first, last = first_slot * padded, last_slot * padded
        for row_start in range(first, last, 2 * TILE):
            tile = row_start // TILE
            both = [
                dot(coeffs[tile + index], picked[tile + index]).reshape(2 * fold, TILE, width)
                for index in range(2)
            ]
            partial[:, row_start : row_start + 2 * TILE, :] = jnp.concatenate(both, 1).astype(BF16)
        rows = slice(first, last)
        real = jnp.concatenate([partial[index, rows] for index in range(fold)], 1)
        imag = jnp.concatenate([partial[fold + index, rows] for index in range(fold)], 1)
        return dot(real, final_real) + dot(imag, final_imag)

    gives = [
        pltpu.make_async_remote_copy(
            src_ref=outgoing.at[offset],
            dst_ref=incoming.at[offset],
            send_sem=give_send.at[offset],
            recv_sem=give_recv.at[offset],
            device_id=device(peers - offset),
            device_id_type=pl.DeviceIdType.MESH,
        )
        for offset in range(1, peers)
    ]
    middle = peers // 2
    result = products(middle, peers)
    outgoing[middle:] = result.reshape(peers - middle, padded, 2 * out_width).astype(BF16)
    for give in gives[middle - 1 :]:
        give.start()
    result = products(0, middle)
    outgoing[:middle] = result.reshape(middle, padded, 2 * out_width).astype(BF16)
    for give in gives[: middle - 1]:
        give.start()
    answer = result[:padded]
    for offset in list(range(middle, peers)) + list(range(1, middle)):
        gives[offset - 1].wait_recv()
        answer = answer + incoming[offset].astype(F32)
    answer = answer.astype(out_ref.dtype)
    out_ref[0, 0] = answer[:count, :out_width]
    out_ref[1, 0] = answer[:count, out_width:]
    for copy in asks + gives:
        copy.wait_send()


def fused(mode_size, group_size, padded, arguments):
    stem_slice, column, row, mode, final, row_labels, mode_labels, requests = arguments
    peers = mode_size * group_size
    row_count, width = stem_slice.shape[2:]
    order = mode.shape[1]
    sub = order // peers
    fold = final.shape[1] // width
    out_width = final.shape[2]
    count = requests.shape[1]
    total = peers * padded
    terms = 2 * sub
    span = terms * TILE
    steps = row_count // row.shape[1] // ROWS_STEP
    row_labels = row_labels.reshape(1, -1)
    mode_labels = mode_labels.reshape(1, -1)
    dma = pltpu.SemaphoreType.DMA
    return pl.pallas_call(
        functools.partial(fused_kernel, mode_size, group_size),
        out_shape=pltpu.VMEM((2, 1, count, out_width), BF16),
        in_specs=[pl.BlockSpec(memory_space=pltpu.HBM)] * 8,
        out_specs=pl.BlockSpec(memory_space=pltpu.VMEM),
        scratch_shapes=[
            pltpu.VMEM((2, row_count, width), BF16),
            pltpu.VMEM(column.shape, BF16),
            pltpu.VMEM(row.shape, BF16),
            pltpu.VMEM(mode.shape, BF16),
            pltpu.VMEM(final.shape, BF16),
            pltpu.VMEM(row_labels.shape, jnp.int32),
            pltpu.VMEM(mode_labels.shape, jnp.int32),
            pltpu.VMEM(requests.shape, jnp.int32),
            pltpu.VMEM((peers, width), jnp.int32),
            pltpu.VMEM((terms, row_count // sub, width), BF16),
            pltpu.VMEM((total // TILE, span, width), BF16),
            pltpu.VMEM((total // TILE, 2 * fold * TILE, span), BF16),
            pltpu.VMEM((2 * fold, total, width), BF16),
            pltpu.VMEM((peers, padded, 2 * out_width), BF16),
            pltpu.VMEM((peers, padded, 2 * out_width), BF16),
            dma((7,)),
            dma((steps,)),
            dma((peers,)),
            dma((peers,)),
            dma((peers,)),
            dma((peers,)),
        ],
        compiler_params=pltpu.CompilerParams(
            collective_id=0, has_side_effects=True, vmem_limit_bytes=60 * 1024 * 1024
        ),
    )(stem_slice, column, row, mode, final, row_labels, mode_labels, requests)


def complex_table(weight):
    real_part = weight[0]
    imag_part = weight[1]
    return jnp.stack([jnp.stack([real_part, imag_part], 1), jnp.stack([-imag_part, real_part], 1)])


def relabel(weight, labels):
    label_count = labels.shape[0]
    onehot = (labels[:, None] == jnp.arange(label_count, dtype=jnp.int32)[None, :]).astype(
        jnp.float32
    )
    relabelled = jnp.einsum(
        "ji,zjn->zin", onehot, weight.astype(jnp.float32), precision=lax.Precision.HIGHEST
    )
    return complex_table(relabelled.astype(jnp.bfloat16))


def swapped(
    stem_slice,
    column_branch,
    row_branch,
    mode_branch,
    final_branch,
    row_labels,
    mode_labels,
    requests,
):
    local_block = stem_slice[:, 0]
    row_count = local_block.shape[1]
    col_width = local_block.shape[2]
    first_mixed = jnp.einsum(
        "zlc,zcwk->wlk",
        local_block,
        complex_table(column_branch),
        preferred_element_type=jnp.float32,
    ).astype(jnp.bfloat16)
    grouped = first_mixed.reshape(2, row_count // col_width, col_width, col_width)
    second = jnp.einsum(
        "zgjc,zjwk->wgkc",
        grouped,
        relabel(row_branch, row_labels),
        preferred_element_type=jnp.float32,
    ).astype(jnp.bfloat16)
    peer_count = lax.axis_size(("mode", "group"))
    order_size = mode_branch.shape[1]
    sub_rows = order_size // peer_count
    blocks = row_count // order_size
    mode_table = relabel(mode_branch, mode_labels).reshape(2, peer_count, sub_rows, 2, order_size)
    shaped = second.reshape(2, peer_count, blocks, sub_rows, col_width)
    mode_mixed = jnp.einsum(
        "zqhsc,zqswk->whkc",
        lax.all_to_all(shaped, ("mode", "group"), split_axis=1, concat_axis=1, tiled=True),
        mode_table,
        preferred_element_type=jnp.float32,
    ).astype(jnp.bfloat16)
    stem_rows = mode_mixed.reshape(2, row_count // 8, 8 * col_width)
    row_total = stem_rows.shape[1]
    wanted = requests[0]
    owner_index = wanted // row_total
    row_index = wanted - owner_index * row_total
    peer_ids = jnp.arange(peer_count, dtype=jnp.int32)
    onehot = (owner_index[:, None] == peer_ids[None, :]).astype(jnp.int32)
    slot_rank = jnp.sum((jnp.cumsum(onehot, axis=0) - onehot) * onehot, axis=1)
    flat_slot = owner_index * CAPACITY + slot_rank
    send_rows = (
        jnp.full((peer_count * CAPACITY,), -1, jnp.int32)
        .at[flat_slot]
        .set(row_index)
        .reshape(peer_count, CAPACITY)
    )
    asked_rows = lax.all_to_all(
        send_rows, ("mode", "group"), split_axis=0, concat_axis=0, tiled=True
    )
    safe_rows = jnp.maximum(asked_rows, 0).reshape(-1)
    final_table = complex_table(final_branch)
    results = jnp.einsum(
        "zlr,zrwk->wlk", stem_rows, final_table, preferred_element_type=jnp.float32
    ).astype(jnp.bfloat16)
    picked = jnp.take(results, safe_rows, axis=1).reshape(2, peer_count, CAPACITY, results.shape[2])
    returned = lax.all_to_all(picked, ("mode", "group"), split_axis=1, concat_axis=1, tiled=True)
    amplitudes = jnp.take(
        returned.reshape(2, peer_count * CAPACITY, results.shape[2]), flat_slot, axis=1
    )
    return amplitudes[:, None]


def per_device(mode_size, group_size, *arguments):
    stem_slice, _, row, mode, final, _, _, requests = arguments
    peers = mode_size * group_size
    row_count, width = stem_slice.shape[2:]
    padded = -(-requests.shape[1] // 16) * 16
    fits = (
        peers == TILE
        and padded <= width
        and row.shape[1] == width
        and mode.shape[1] % (16 * peers) == 0
        and row_count % (ROWS_STEP * width) == 0
        and 2 * peers * padded * final.shape[2] < stem_slice.size
    )
    if fits:
        return fused(mode_size, group_size, padded, arguments)
    return swapped(*arguments)


def solution(mesh):
    return jax.shard_map(
        functools.partial(per_device, mesh.shape["mode"], mesh.shape["group"]),
        mesh=mesh,
        in_specs=(
            P(None, ("cuts", "batch"), ("mode", "group"), None),
            P(),
            P(),
            P(),
            P(),
            P(),
            P(),
            P("batch", ("mode", "group")),
        ),
        out_specs=P(None, ("cuts", "batch"), ("mode", "group"), None),
        check_vma=False,
    )
```

```python
import functools

import jax
import jax.numpy as jnp
from jax import lax
from jax.experimental import pallas as pl
from jax.experimental.pallas import tpu as pltpu
from jax.sharding import PartitionSpec as P

CAPACITY = 8
TILE = 8
ROWS_STEP = 2

F32 = jnp.float32
BF16 = jnp.bfloat16


def dot(left, right):
    return jnp.dot(left, right, preferred_element_type=F32)


def dot_t(left, right):
    return lax.dot_general(left, right, (((1,), (1,)), ((), ())), preferred_element_type=F32)


def iota(shape, dim):
    return lax.broadcasted_iota(jnp.int32, shape, dim)


def complex_rows(real, imag, axis):
    return jnp.concatenate([real, -imag], axis), jnp.concatenate([imag, real], axis)


def fused_kernel(
    mode_size,
    group_size,
    stem_hbm,
    column_hbm,
    row_hbm,
    mode_hbm,
    final_hbm,
    row_labels_hbm,
    mode_labels_hbm,
    requests_hbm,
    out_ref,
    stem,
    column,
    row,
    mode,
    final,
    row_labels,
    mode_labels,
    wanted,
    asked,
    spread,
    picked,
    coeffs,
    partial,
    outgoing,
    incoming,
    load_sem,
    stem_sem,
    ask_send,
    ask_recv,
    give_send,
    give_recv,
):
    peers = mode_size * group_size
    row_count, width = stem.shape[1], stem.shape[2]
    row_order = row.shape[1]
    order = mode.shape[1]
    sub = order // peers
    heads = row_order // sub
    groups = row_count // row_order
    length = final.shape[1]
    fold = length // width
    out_width = final.shape[2]
    count = wanted.shape[1]
    padded = outgoing.shape[1]
    blocks = row_count // sub
    row_blocks = order // fold
    terms = 2 * sub
    span = terms * TILE

    mode_index = lax.axis_index("mode")
    group_index = lax.axis_index("group")
    me = mode_index * group_size + group_index

    def device(offset):
        peer = me
        bit = 1
        while bit <= offset:
            if offset & bit:
                peer = peer + bit - 2 * bit * lax.rem(peer // bit, 2)
            bit *= 2
        return {"mode": peer // group_size, "group": lax.rem(peer, group_size)}

    barrier = pltpu.get_barrier_semaphore()
    for offset in range(1, peers):
        pl.semaphore_signal(
            barrier, inc=1, device_id=device(offset), device_id_type=pl.DeviceIdType.MESH
        )

    small = [
        pltpu.make_async_copy(source, target, load_sem.at[index])
        for index, (source, target) in enumerate(
            (
                (requests_hbm, wanted),
                (column_hbm, column),
                (row_hbm, row),
                (row_labels_hbm, row_labels),
                (mode_hbm, mode),
                (mode_labels_hbm, mode_labels),
                (final_hbm, final),
            )
        )
    ]
    step_rows = ROWS_STEP * row_order
    stem_loads = [
        pltpu.make_async_copy(
            stem_hbm.at[:, 0, pl.ds(step * step_rows, step_rows), :],
            stem.at[:, pl.ds(step * step_rows, step_rows), :],
            stem_sem.at[step],
        )
        for step in range(groups // ROWS_STEP)
    ]
    for load in small[:4] + stem_loads + small[4:]:
        load.start()

    small[0].wait()
    asked[0:1, :] = jnp.zeros((1, width), jnp.int32)
    asked[0:1, 0:count] = wanted[...]
    for load in small[1:4] + stem_loads:
        load.wait()

    column_real, column_imag = complex_rows(column[0], column[1], 0)
    column_table = jnp.concatenate([column_real, column_imag], 1)
    chosen = (iota((row_order, row_order), 0) == row_labels[...]).astype(BF16)
    cube = (sub, heads, row_order)
    swap_rows = (
        (iota(cube, 1) * sub + iota(cube, 0) == iota(cube, 2))
        .astype(F32)
        .reshape(row_order, row_order)
        .astype(BF16)
    )
    row_real = dot_t(swap_rows, dot(chosen, row[0]).astype(BF16)).astype(BF16)
    row_imag = dot_t(swap_rows, dot(chosen, row[1]).astype(BF16)).astype(BF16)
    row_table = jnp.concatenate(complex_rows(row_real, row_imag, 1), 0)

    def mix(step):
        rows = pl.ds(step * step_rows, step_rows)
        operand = jnp.concatenate([stem[0, rows, :], stem[1, rows, :]], 1)
        mixed = dot(operand, column_table).astype(BF16)
        pieces = []
        for index in range(ROWS_STEP):
            piece = mixed[index * row_order : (index + 1) * row_order]
            pieces.append(jnp.concatenate([piece[:, :width], piece[:, width:]], 0))
        result = dot(row_table, jnp.concatenate(pieces, 1))
        result = [
            result[:, index * width : (index + 1) * width].reshape(terms, heads, width)
            for index in range(ROWS_STEP)
        ]
        first = step * ROWS_STEP * heads
        spread[:, first : first + ROWS_STEP * heads, :] = jnp.concatenate(result, 1).astype(BF16)

    steps = groups // ROWS_STEP
    for step in range(steps // 2):
        mix(step)

    pl.semaphore_wait(barrier, peers - 1)
    asks = [
        pltpu.make_async_remote_copy(
            src_ref=asked.at[pl.ds(0, 1), :],
            dst_ref=asked.at[pl.ds(offset, 1), :],
            send_sem=ask_send.at[offset],
            recv_sem=ask_recv.at[offset],
            device_id=device(offset),
            device_id_type=pl.DeviceIdType.MESH,
        )
        for offset in range(1, peers)
    ]
    for ask in asks:
        ask.start()
    for load in small[4:]:
        load.wait()

    for step in range(steps // 2, steps):
        mix(step)

    own = (iota((sub, order), 0) + me * sub == mode_labels[...]).astype(BF16)
    mode_real, mode_imag = dot(own, mode[0]), dot(own, mode[1])
    cube = (terms, TILE, terms)
    repeat = (iota(cube, 0) == iota(cube, 2)).astype(F32).reshape(span, terms).astype(BF16)
    mode_table = dot(repeat, jnp.concatenate([mode_real, mode_imag], 0).astype(BF16)).astype(BF16)

    for ask in asks:
        ask.wait_recv()
    ids = asked[...]
    block_ids = jnp.transpose(lax.div(ids, row_blocks).astype(F32))
    order_ids = jnp.transpose((lax.rem(ids, row_blocks) * fold).astype(F32))

    final_real = jnp.concatenate([final[0], final[1]], 1)
    final_imag = jnp.concatenate([-final[1], final[0]], 1)

    def products(first_slot, last_slot):
        first, last = first_slot * padded, last_slot * padded
        rows = last - first
        tiles = rows // TILE
        first_tile = first // TILE

        def column_of(values, lanes):
            return jnp.concatenate(
                [
                    jnp.broadcast_to(values[:padded, slot : slot + 1], (padded, lanes))
                    for slot in range(first_slot, last_slot)
                ],
                0,
            )

        def paired(one, other):
            lanes = one.shape[1]
            both = [part.reshape(tiles, TILE, lanes) for part in (one, other)]
            return jnp.concatenate(both, 1).astype(BF16)

        pick = (column_of(block_ids, blocks) == iota((rows, blocks), 1).astype(F32)).astype(BF16)
        for term in range(0, terms, 2):
            found = dot(pick, jnp.concatenate([spread[term], spread[term + 1]], 1))
            picked[first_tile : first_tile + tiles, term * TILE : (term + 2) * TILE, :] = paired(
                found[:, :width], found[:, width:]
            )

        order_column = column_of(order_ids, order)
        lane = iota((rows, order), 1).astype(F32)
        same = (iota((TILE, span), 1) & (TILE - 1)) == iota((TILE, span), 0)
        same = jnp.broadcast_to(same[None], (tiles, TILE, span)).reshape(rows, span)

        def coefficients(index):
            at = (order_column + float(index) == lane).astype(BF16)
            return jnp.where(same, dot_t(at, mode_table), 0.0)

        for index in range(0, fold, 2):
            pair = paired(coefficients(index), coefficients(index + 1))
            real, imag = pair[:, :, : span // 2], pair[:, :, span // 2 :]
            for half, both in enumerate(((real, -imag), (imag, real))):
                start = (half * fold + index) * TILE
                coeffs[
                    first_tile : first_tile + tiles, start : start + 2 * TILE, :
                ] = jnp.concatenate(both, 2)

        for row_start in range(first, last, 2 * TILE):
            tile = row_start // TILE
            both = [
                dot(coeffs[tile + index], picked[tile + index]).reshape(2 * fold, TILE, width)
                for index in range(2)
            ]
            partial[:, row_start : row_start + 2 * TILE, :] = jnp.concatenate(both, 1).astype(BF16)
        real = jnp.concatenate([partial[index, first:last] for index in range(fold)], 1)
        imag = jnp.concatenate([partial[fold + index, first:last] for index in range(fold)], 1)
        return dot(real, final_real) + dot(imag, final_imag)

    gives = [
        pltpu.make_async_remote_copy(
            src_ref=outgoing.at[offset],
            dst_ref=incoming.at[offset],
            send_sem=give_send.at[offset],
            recv_sem=give_recv.at[offset],
            device_id=device(offset),
            device_id_type=pl.DeviceIdType.MESH,
        )
        for offset in range(1, peers)
    ]
    middle = peers // 2
    result = products(middle, peers)
    outgoing[middle:] = result.reshape(peers - middle, padded, 2 * out_width).astype(BF16)
    for give in gives[middle - 1 :]:
        give.start()
    result = products(0, middle)
    outgoing[:middle] = result.reshape(middle, padded, 2 * out_width).astype(BF16)
    for give in gives[: middle - 1]:
        give.start()
    answer = result[:padded]
    for offset in list(range(middle, peers)) + list(range(1, middle)):
        gives[offset - 1].wait_recv()
        answer = answer + incoming[offset].astype(F32)
    answer = answer.astype(out_ref.dtype)
    out_ref[0, 0] = answer[:count, :out_width]
    out_ref[1, 0] = answer[:count, out_width:]
    for copy in asks + gives:
        copy.wait_send()


def fused(mode_size, group_size, padded, arguments):
    stem_slice, column, row, mode, final, row_labels, mode_labels, requests = arguments
    peers = mode_size * group_size
    row_count, width = stem_slice.shape[2:]
    order = mode.shape[1]
    sub = order // peers
    fold = final.shape[1] // width
    out_width = final.shape[2]
    count = requests.shape[1]
    total = peers * padded
    terms = 2 * sub
    span = terms * TILE
    steps = row_count // row.shape[1] // ROWS_STEP
    row_labels = row_labels.reshape(1, -1)
    mode_labels = mode_labels.reshape(1, -1)
    dma = pltpu.SemaphoreType.DMA
    return pl.pallas_call(
        functools.partial(fused_kernel, mode_size, group_size),
        out_shape=pltpu.VMEM((2, 1, count, out_width), BF16),
        in_specs=[pl.BlockSpec(memory_space=pltpu.HBM)] * 8,
        out_specs=pl.BlockSpec(memory_space=pltpu.VMEM),
        scratch_shapes=[
            pltpu.VMEM((2, row_count, width), BF16),
            pltpu.VMEM(column.shape, BF16),
            pltpu.VMEM(row.shape, BF16),
            pltpu.VMEM(mode.shape, BF16),
            pltpu.VMEM(final.shape, BF16),
            pltpu.VMEM(row_labels.shape, jnp.int32),
            pltpu.VMEM(mode_labels.shape, jnp.int32),
            pltpu.VMEM(requests.shape, jnp.int32),
            pltpu.VMEM((peers, width), jnp.int32),
            pltpu.VMEM((terms, row_count // sub, width), BF16),
            pltpu.VMEM((total // TILE, span, width), BF16),
            pltpu.VMEM((total // TILE, 2 * fold * TILE, span), BF16),
            pltpu.VMEM((2 * fold, total, width), BF16),
            pltpu.VMEM((peers, padded, 2 * out_width), BF16),
            pltpu.VMEM((peers, padded, 2 * out_width), BF16),
            dma((7,)),
            dma((steps,)),
            dma((peers,)),
            dma((peers,)),
            dma((peers,)),
            dma((peers,)),
        ],
        compiler_params=pltpu.CompilerParams(
            collective_id=0, has_side_effects=True, vmem_limit_bytes=60 * 1024 * 1024
        ),
    )(stem_slice, column, row, mode, final, row_labels, mode_labels, requests)


def complex_table(weight):
    real_part = weight[0]
    imag_part = weight[1]
    return jnp.stack([jnp.stack([real_part, imag_part], 1), jnp.stack([-imag_part, real_part], 1)])


def relabel(weight, labels):
    label_count = labels.shape[0]
    onehot = (labels[:, None] == jnp.arange(label_count, dtype=jnp.int32)[None, :]).astype(
        jnp.float32
    )
    relabelled = jnp.einsum(
        "ji,zjn->zin", onehot, weight.astype(jnp.float32), precision=lax.Precision.HIGHEST
    )
    return complex_table(relabelled.astype(jnp.bfloat16))


def swapped(
    stem_slice,
    column_branch,
    row_branch,
    mode_branch,
    final_branch,
    row_labels,
    mode_labels,
    requests,
):
    local_block = stem_slice[:, 0]
    row_count = local_block.shape[1]
    col_width = local_block.shape[2]
    first_mixed = jnp.einsum(
        "zlc,zcwk->wlk",
        local_block,
        complex_table(column_branch),
        preferred_element_type=jnp.float32,
    ).astype(jnp.bfloat16)
    grouped = first_mixed.reshape(2, row_count // col_width, col_width, col_width)
    second = jnp.einsum(
        "zgjc,zjwk->wgkc",
        grouped,
        relabel(row_branch, row_labels),
        preferred_element_type=jnp.float32,
    ).astype(jnp.bfloat16)
    peer_count = lax.axis_size(("mode", "group"))
    order_size = mode_branch.shape[1]
    sub_rows = order_size // peer_count
    blocks = row_count // order_size
    mode_table = relabel(mode_branch, mode_labels).reshape(2, peer_count, sub_rows, 2, order_size)
    shaped = second.reshape(2, peer_count, blocks, sub_rows, col_width)
    mode_mixed = jnp.einsum(
        "zqhsc,zqswk->whkc",
        lax.all_to_all(shaped, ("mode", "group"), split_axis=1, concat_axis=1, tiled=True),
        mode_table,
        preferred_element_type=jnp.float32,
    ).astype(jnp.bfloat16)
    stem_rows = mode_mixed.reshape(2, row_count // 8, 8 * col_width)
    row_total = stem_rows.shape[1]
    wanted = requests[0]
    owner_index = wanted // row_total
    row_index = wanted - owner_index * row_total
    peer_ids = jnp.arange(peer_count, dtype=jnp.int32)
    onehot = (owner_index[:, None] == peer_ids[None, :]).astype(jnp.int32)
    slot_rank = jnp.sum((jnp.cumsum(onehot, axis=0) - onehot) * onehot, axis=1)
    flat_slot = owner_index * CAPACITY + slot_rank
    send_rows = (
        jnp.full((peer_count * CAPACITY,), -1, jnp.int32)
        .at[flat_slot]
        .set(row_index)
        .reshape(peer_count, CAPACITY)
    )
    asked_rows = lax.all_to_all(
        send_rows, ("mode", "group"), split_axis=0, concat_axis=0, tiled=True
    )
    safe_rows = jnp.maximum(asked_rows, 0).reshape(-1)
    final_table = complex_table(final_branch)
    results = jnp.einsum(
        "zlr,zrwk->wlk", stem_rows, final_table, preferred_element_type=jnp.float32
    ).astype(jnp.bfloat16)
    picked = jnp.take(results, safe_rows, axis=1).reshape(2, peer_count, CAPACITY, results.shape[2])
    returned = lax.all_to_all(picked, ("mode", "group"), split_axis=1, concat_axis=1, tiled=True)
    amplitudes = jnp.take(
        returned.reshape(2, peer_count * CAPACITY, results.shape[2]), flat_slot, axis=1
    )
    return amplitudes[:, None]


def per_device(mode_size, group_size, *arguments):
    stem_slice, _, row, mode, final, _, _, requests = arguments
    peers = mode_size * group_size
    row_count, width = stem_slice.shape[2:]
    padded = -(-requests.shape[1] // 16) * 16
    fits = (
        peers == TILE
        and padded <= width
        and row.shape[1] == width
        and mode.shape[1] % (16 * peers) == 0
        and row_count % (ROWS_STEP * width) == 0
        and 2 * peers * padded * final.shape[2] < stem_slice.size
    )
    if fits:
        return fused(mode_size, group_size, padded, arguments)
    return swapped(*arguments)


def solution(mesh):
    return jax.shard_map(
        functools.partial(per_device, mesh.shape["mode"], mesh.shape["group"]),
        mesh=mesh,
        in_specs=(
            P(None, ("cuts", "batch"), ("mode", "group"), None),
            P(),
            P(),
            P(),
            P(),
            P(),
            P(),
            P("batch", ("mode", "group")),
        ),
        out_specs=P(None, ("cuts", "batch"), ("mode", "group"), None),
        check_vma=False,
    )
```

```python
import functools

import jax
import jax.numpy as jnp
from jax import lax
from jax.experimental import pallas as pl
from jax.experimental.pallas import tpu as pltpu
from jax.sharding import PartitionSpec as P

CAPACITY = 8
TILE = 8
ROWS_STEP = 2

F32 = jnp.float32
BF16 = jnp.bfloat16


def dot(left, right):
    return jnp.dot(left, right, preferred_element_type=F32)


def dot_t(left, right):
    return lax.dot_general(left, right, (((0,), (1,)), ((), ())), preferred_element_type=F32)


def iota(shape, dim):
    return lax.broadcasted_iota(jnp.int32, shape, dim)


def complex_rows(real, imag, axis):
    return jnp.concatenate([real, -imag], axis), jnp.concatenate([imag, real], axis)


def fused_kernel(
    mode_size,
    group_size,
    stem_hbm,
    column_hbm,
    row_hbm,
    mode_hbm,
    final_hbm,
    row_labels_hbm,
    mode_labels_hbm,
    requests_hbm,
    out_ref,
    stem,
    column,
    row,
    mode,
    final,
    row_labels,
    mode_labels,
    wanted,
    asked,
    indices,
    spread,
    coeffs,
    partial,
    outgoing,
    incoming,
    load_sem,
    index_sem,
    stem_sem,
    ask_send,
    ask_recv,
    give_send,
    give_recv,
):
    peers = mode_size * group_size
    row_count, width = stem.shape[1], stem.shape[2]
    row_order = row.shape[1]
    order = mode.shape[1]
    sub = order // peers
    heads = row_order // sub
    groups = row_count // row_order
    length = final.shape[1]
    fold = length // width
    out_width = final.shape[2]
    count = wanted.shape[1]
    padded = outgoing.shape[1]
    blocks = row_count // sub
    row_blocks = order // fold
    terms = 2 * sub
    span = terms * TILE

    mode_index = lax.axis_index("mode")
    group_index = lax.axis_index("group")
    me = mode_index * group_size + group_index

    def device(offset):
        peer = me
        bit = 1
        while bit <= offset:
            if offset & bit:
                peer = peer + bit - 2 * bit * lax.rem(peer // bit, 2)
            bit *= 2
        return {"mode": peer // group_size, "group": lax.rem(peer, group_size)}

    barrier = pltpu.get_barrier_semaphore()
    for offset in range(1, peers):
        pl.semaphore_signal(
            barrier, inc=1, device_id=device(offset), device_id_type=pl.DeviceIdType.MESH
        )

    small = [
        pltpu.make_async_copy(source, target, load_sem.at[index])
        for index, (source, target) in enumerate(
            (
                (requests_hbm, wanted),
                (column_hbm, column),
                (row_hbm, row),
                (row_labels_hbm, row_labels),
                (mode_hbm, mode),
                (mode_labels_hbm, mode_labels),
                (final_hbm, final),
            )
        )
    ]
    step_rows = ROWS_STEP * row_order
    stem_loads = [
        pltpu.make_async_copy(
            stem_hbm.at[:, 0, pl.ds(step * step_rows, step_rows), :],
            stem.at[:, pl.ds(step * step_rows, step_rows), :],
            stem_sem.at[step],
        )
        for step in range(groups // ROWS_STEP)
    ]
    for load in small[:4] + stem_loads + small[4:]:
        load.start()

    small[0].wait()
    asked[0:2, :] = jnp.zeros((2, width), jnp.int32)
    asked[0:1, 0:count] = lax.div(wanted[...], row_blocks)
    asked[1:2, 0:count] = lax.rem(wanted[...], row_blocks)
    pl.semaphore_wait(barrier, peers - 1)
    asks = [
        pltpu.make_async_remote_copy(
            src_ref=asked.at[pl.ds(0, 2), :],
            dst_ref=asked.at[pl.ds(2 * offset, 2), :],
            send_sem=ask_send.at[offset],
            recv_sem=ask_recv.at[offset],
            device_id=device(offset),
            device_id_type=pl.DeviceIdType.MESH,
        )
        for offset in range(1, peers)
    ]
    for ask in asks:
        ask.start()
    for load in small[1:] + stem_loads:
        load.wait()

    column_real, column_imag = complex_rows(column[0], column[1], 0)
    column_table = jnp.concatenate([column_real, column_imag], 1)
    chosen = (iota((row_order, row_order), 0) == row_labels[...]).astype(BF16)

    def relabelled(weight):
        return dot_t(weight, chosen).astype(BF16)

    row_table = jnp.concatenate(
        [
            half.reshape(heads, sub, 2 * row_order)
            for half in complex_rows(relabelled(row[0]), relabelled(row[1]), 1)
        ],
        1,
    ).reshape(2 * row_order, 2 * row_order)

    def mix(step):
        rows = pl.ds(step * step_rows, step_rows)
        operand = jnp.concatenate([stem[0, rows, :], stem[1, rows, :]], 1)
        mixed = dot(operand, column_table).astype(BF16)
        pieces = []
        for index in range(ROWS_STEP):
            piece = mixed[index * row_order : (index + 1) * row_order]
            pieces.append(jnp.concatenate([piece[:, :width], piece[:, width:]], 0))
        result = dot(row_table, jnp.concatenate(pieces, 1))
        for index in range(ROWS_STEP):
            first = (step * ROWS_STEP + index) * heads
            spread[first : first + heads] = (
                result[:, index * width : (index + 1) * width]
                .reshape(heads, terms, width)
                .astype(BF16)
            )

    for step in range(groups // ROWS_STEP):
        mix(step)

    own = (iota((sub, order), 0) + me * sub == mode_labels[...]).astype(BF16)
    mode_real, mode_imag = dot(own, mode[0]), dot(own, mode[1])
    lane = iota((terms, span), 1)
    repeat = functools.reduce(
        jnp.logical_or,
        [lane == iota((terms, span), 0) + place * terms for place in range(TILE)],
    ).astype(BF16)
    blocks_of = jnp.concatenate(
        [
            dot(jnp.transpose(half).astype(BF16), repeat).reshape(row_blocks, fold, span)
            for half in complex_rows(mode_real, mode_imag, 0)
        ],
        1,
    )
    lane = iota(blocks_of.shape, 2)
    for place in range(TILE):
        inside = (lane >= place * terms) & (lane < (place + 1) * terms)
        coeffs[place] = jnp.where(inside, blocks_of, 0.0).astype(BF16)

    final_real = jnp.concatenate([final[0], final[1]], 1)
    final_imag = jnp.concatenate([-final[1], final[0]], 1)

    for ask in asks:
        ask.wait_recv()
    to_scalars = pltpu.make_async_copy(asked, indices, index_sem)
    to_scalars.start()
    to_scalars.wait()

    def products(first_slot, last_slot):
        first, last = first_slot * padded, last_slot * padded
        rows = last - first
        for start in range(first, last, TILE):
            left, right = [], []
            for place in range(TILE):
                slot, entry = (start + place) // padded, (start + place) % padded
                left.append(coeffs[place, indices[2 * slot + 1, entry]])
                right.append(spread[indices[2 * slot, entry]])
            partial[start * 2 * fold : (start + TILE) * 2 * fold, :] = dot(
                jnp.concatenate(left, 0), jnp.concatenate(right, 0)
            )
        pieces = [
            partial[pl.ds(first * 2 * fold + index, rows, stride=2 * fold), :].astype(BF16)
            for index in range(2 * fold)
        ]
        real = jnp.concatenate(pieces[:fold], 1)
        imag = jnp.concatenate(pieces[fold:], 1)
        return dot(real, final_real) + dot(imag, final_imag)

    gives = [
        pltpu.make_async_remote_copy(
            src_ref=outgoing.at[offset],
            dst_ref=incoming.at[offset],
            send_sem=give_send.at[offset],
            recv_sem=give_recv.at[offset],
            device_id=device(offset),
            device_id_type=pl.DeviceIdType.MESH,
        )
        for offset in range(1, peers)
    ]
    middle = peers // 2
    result = products(middle, peers)
    outgoing[middle:] = result.reshape(peers - middle, padded, 2 * out_width).astype(BF16)
    for give in gives[middle - 1 :]:
        give.start()
    result = products(0, middle)
    outgoing[:middle] = result.reshape(middle, padded, 2 * out_width).astype(BF16)
    for give in gives[: middle - 1]:
        give.start()
    answer = result[:padded]
    for offset in list(range(middle, peers)) + list(range(1, middle)):
        gives[offset - 1].wait_recv()
        answer = answer + incoming[offset].astype(F32)
    answer = answer.astype(out_ref.dtype)
    out_ref[0, 0] = answer[:count, :out_width]
    out_ref[1, 0] = answer[:count, out_width:]
    for copy in asks + gives:
        copy.wait_send()


def fused(mode_size, group_size, padded, arguments):
    stem_slice, column, row, mode, final, row_labels, mode_labels, requests = arguments
    peers = mode_size * group_size
    row_count, width = stem_slice.shape[2:]
    order = mode.shape[1]
    sub = order // peers
    fold = final.shape[1] // width
    out_width = final.shape[2]
    count = requests.shape[1]
    total = peers * padded
    terms = 2 * sub
    span = terms * TILE
    steps = row_count // row.shape[1] // ROWS_STEP
    row_labels = row_labels.reshape(1, -1)
    mode_labels = mode_labels.reshape(1, -1)
    dma = pltpu.SemaphoreType.DMA
    return pl.pallas_call(
        functools.partial(fused_kernel, mode_size, group_size),
        out_shape=pltpu.VMEM((2, 1, count, out_width), BF16),
        in_specs=[pl.BlockSpec(memory_space=pltpu.HBM)] * 8,
        out_specs=pl.BlockSpec(memory_space=pltpu.VMEM),
        scratch_shapes=[
            pltpu.VMEM((2, row_count, width), BF16),
            pltpu.VMEM(column.shape, BF16),
            pltpu.VMEM(row.shape, BF16),
            pltpu.VMEM(mode.shape, BF16),
            pltpu.VMEM(final.shape, BF16),
            pltpu.VMEM(row_labels.shape, jnp.int32),
            pltpu.VMEM(mode_labels.shape, jnp.int32),
            pltpu.VMEM(requests.shape, jnp.int32),
            pltpu.VMEM((2 * peers, width), jnp.int32),
            pltpu.SMEM((2 * peers, width), jnp.int32),
            pltpu.VMEM((row_count // sub, terms, width), BF16),
            pltpu.VMEM((TILE, order // fold, 2 * fold, span), BF16),
            pltpu.VMEM((total * 2 * fold, width), F32),
            pltpu.VMEM((peers, padded, 2 * out_width), BF16),
            pltpu.VMEM((peers, padded, 2 * out_width), BF16),
            dma((7,)),
            dma,
            dma((steps,)),
            dma((peers,)),
            dma((peers,)),
            dma((peers,)),
            dma((peers,)),
        ],
        compiler_params=pltpu.CompilerParams(
            collective_id=0, has_side_effects=True, vmem_limit_bytes=60 * 1024 * 1024
        ),
    )(stem_slice, column, row, mode, final, row_labels, mode_labels, requests)


def complex_table(weight):
    real_part = weight[0]
    imag_part = weight[1]
    return jnp.stack([jnp.stack([real_part, imag_part], 1), jnp.stack([-imag_part, real_part], 1)])


def relabel(weight, labels):
    label_count = labels.shape[0]
    onehot = (labels[:, None] == jnp.arange(label_count, dtype=jnp.int32)[None, :]).astype(
        jnp.float32
    )
    relabelled = jnp.einsum(
        "ji,zjn->zin", onehot, weight.astype(jnp.float32), precision=lax.Precision.HIGHEST
    )
    return complex_table(relabelled.astype(jnp.bfloat16))


def swapped(
    stem_slice,
    column_branch,
    row_branch,
    mode_branch,
    final_branch,
    row_labels,
    mode_labels,
    requests,
):
    local_block = stem_slice[:, 0]
    row_count = local_block.shape[1]
    col_width = local_block.shape[2]
    first_mixed = jnp.einsum(
        "zlc,zcwk->wlk",
        local_block,
        complex_table(column_branch),
        preferred_element_type=jnp.float32,
    ).astype(jnp.bfloat16)
    grouped = first_mixed.reshape(2, row_count // col_width, col_width, col_width)
    second = jnp.einsum(
        "zgjc,zjwk->wgkc",
        grouped,
        relabel(row_branch, row_labels),
        preferred_element_type=jnp.float32,
    ).astype(jnp.bfloat16)
    peer_count = lax.axis_size(("mode", "group"))
    order_size = mode_branch.shape[1]
    sub_rows = order_size // peer_count
    blocks = row_count // order_size
    mode_table = relabel(mode_branch, mode_labels).reshape(2, peer_count, sub_rows, 2, order_size)
    shaped = second.reshape(2, peer_count, blocks, sub_rows, col_width)
    mode_mixed = jnp.einsum(
        "zqhsc,zqswk->whkc",
        lax.all_to_all(shaped, ("mode", "group"), split_axis=1, concat_axis=1, tiled=True),
        mode_table,
        preferred_element_type=jnp.float32,
    ).astype(jnp.bfloat16)
    stem_rows = mode_mixed.reshape(2, row_count // 8, 8 * col_width)
    row_total = stem_rows.shape[1]
    wanted = requests[0]
    owner_index = wanted // row_total
    row_index = wanted - owner_index * row_total
    peer_ids = jnp.arange(peer_count, dtype=jnp.int32)
    onehot = (owner_index[:, None] == peer_ids[None, :]).astype(jnp.int32)
    slot_rank = jnp.sum((jnp.cumsum(onehot, axis=0) - onehot) * onehot, axis=1)
    flat_slot = owner_index * CAPACITY + slot_rank
    send_rows = (
        jnp.full((peer_count * CAPACITY,), -1, jnp.int32)
        .at[flat_slot]
        .set(row_index)
        .reshape(peer_count, CAPACITY)
    )
    asked_rows = lax.all_to_all(
        send_rows, ("mode", "group"), split_axis=0, concat_axis=0, tiled=True
    )
    safe_rows = jnp.maximum(asked_rows, 0).reshape(-1)
    final_table = complex_table(final_branch)
    results = jnp.einsum(
        "zlr,zrwk->wlk", stem_rows, final_table, preferred_element_type=jnp.float32
    ).astype(jnp.bfloat16)
    picked = jnp.take(results, safe_rows, axis=1).reshape(2, peer_count, CAPACITY, results.shape[2])
    returned = lax.all_to_all(picked, ("mode", "group"), split_axis=1, concat_axis=1, tiled=True)
    amplitudes = jnp.take(
        returned.reshape(2, peer_count * CAPACITY, results.shape[2]), flat_slot, axis=1
    )
    return amplitudes[:, None]


def per_device(mode_size, group_size, *arguments):
    stem_slice, _, row, mode, final, _, _, requests = arguments
    peers = mode_size * group_size
    row_count, width = stem_slice.shape[2:]
    padded = -(-requests.shape[1] // 16) * 16
    fits = (
        peers == TILE
        and padded <= width
        and row.shape[1] == width
        and mode.shape[1] % (16 * peers) == 0
        and row_count % (ROWS_STEP * width) == 0
        and 2 * peers * padded * final.shape[2] < stem_slice.size
    )
    if fits:
        return fused(mode_size, group_size, padded, arguments)
    return swapped(*arguments)


def solution(mesh):
    return jax.shard_map(
        functools.partial(per_device, mesh.shape["mode"], mesh.shape["group"]),
        mesh=mesh,
        in_specs=(
            P(None, ("cuts", "batch"), ("mode", "group"), None),
            P(),
            P(),
            P(),
            P(),
            P(),
            P(),
            P("batch", ("mode", "group")),
        ),
        out_specs=P(None, ("cuts", "batch"), ("mode", "group"), None),
        check_vma=False,
    )
```

```python
import functools

import jax
import jax.numpy as jnp
from jax import lax
from jax.experimental import pallas as pl
from jax.experimental.pallas import tpu as pltpu
from jax.sharding import PartitionSpec as P

CAPACITY = 8
TILE = 8
ROWS_STEP = 2

F32 = jnp.float32
BF16 = jnp.bfloat16


def dot(left, right):
    return jnp.dot(left, right, preferred_element_type=F32)


def dot_t(left, right):
    return lax.dot_general(left, right, (((0,), (1,)), ((), ())), preferred_element_type=F32)


def iota(shape, dim):
    return lax.broadcasted_iota(jnp.int32, shape, dim)


def complex_rows(real, imag, axis):
    return jnp.concatenate([real, -imag], axis), jnp.concatenate([imag, real], axis)


def fused_kernel(
    mode_size,
    group_size,
    stem_hbm,
    column_hbm,
    row_hbm,
    mode_hbm,
    final_hbm,
    row_labels_hbm,
    mode_labels_hbm,
    requests_hbm,
    out_ref,
    stem,
    column,
    row,
    mode,
    final,
    row_labels,
    mode_labels,
    wanted,
    asked,
    indices,
    spread,
    coeffs,
    partial,
    outgoing,
    incoming,
    load_sem,
    index_sem,
    stem_sem,
    ask_send,
    ask_recv,
    give_send,
    give_recv,
):
    peers = mode_size * group_size
    row_count, width = stem.shape[1], stem.shape[2]
    row_order = row.shape[1]
    order = mode.shape[1]
    sub = order // peers
    heads = row_order // sub
    groups = row_count // row_order
    length = final.shape[1]
    fold = length // width
    out_width = final.shape[2]
    count = wanted.shape[1]
    padded = outgoing.shape[1]
    blocks = row_count // sub
    row_blocks = order // fold
    terms = 2 * sub
    span = terms * TILE

    mode_index = lax.axis_index("mode")
    group_index = lax.axis_index("group")
    me = mode_index * group_size + group_index

    def device(offset):
        peer = me
        bit = 1
        while bit <= offset:
            if offset & bit:
                peer = peer + bit - 2 * bit * lax.rem(peer // bit, 2)
            bit *= 2
        return {"mode": peer // group_size, "group": lax.rem(peer, group_size)}

    barrier = pltpu.get_barrier_semaphore()
    for offset in range(1, peers):
        pl.semaphore_signal(
            barrier, inc=1, device_id=device(offset), device_id_type=pl.DeviceIdType.MESH
        )

    small = [
        pltpu.make_async_copy(source, target, load_sem.at[index])
        for index, (source, target) in enumerate(
            (
                (requests_hbm, wanted),
                (column_hbm, column),
                (row_hbm, row),
                (row_labels_hbm, row_labels),
                (mode_hbm, mode),
                (mode_labels_hbm, mode_labels),
                (final_hbm, final),
            )
        )
    ]
    step_rows = ROWS_STEP * row_order
    stem_loads = [
        pltpu.make_async_copy(
            stem_hbm.at[:, 0, pl.ds(step * step_rows, step_rows), :],
            stem.at[:, pl.ds(step * step_rows, step_rows), :],
            stem_sem.at[step],
        )
        for step in range(groups // ROWS_STEP)
    ]
    for load in small[:4] + stem_loads + small[4:]:
        load.start()

    small[0].wait()
    asked[0:2, :] = jnp.zeros((2, width), jnp.int32)
    asked[0:1, 0:count] = lax.div(wanted[...], row_blocks)
    asked[1:2, 0:count] = lax.rem(wanted[...], row_blocks)
    for load in small[1:4] + stem_loads:
        load.wait()

    column_real, column_imag = complex_rows(column[0], column[1], 0)
    column_table = jnp.concatenate([column_real, column_imag], 1)
    chosen = (iota((row_order, row_order), 0) == row_labels[...]).astype(BF16)

    def relabelled(weight):
        return dot_t(weight, chosen).astype(BF16)

    row_table = jnp.concatenate(
        [
            half.reshape(heads, sub, 2 * row_order)
            for half in complex_rows(relabelled(row[0]), relabelled(row[1]), 1)
        ],
        1,
    ).reshape(2 * row_order, 2 * row_order)

    def mix(step):
        rows = pl.ds(step * step_rows, step_rows)
        operand = jnp.concatenate([stem[0, rows, :], stem[1, rows, :]], 1)
        mixed = dot(operand, column_table).astype(BF16)
        pieces = []
        for index in range(ROWS_STEP):
            piece = mixed[index * row_order : (index + 1) * row_order]
            pieces.append(jnp.concatenate([piece[:, :width], piece[:, width:]], 0))
        result = dot(row_table, jnp.concatenate(pieces, 1))
        for index in range(ROWS_STEP):
            first = (step * ROWS_STEP + index) * heads
            spread[first : first + heads] = (
                result[:, index * width : (index + 1) * width]
                .reshape(heads, terms, width)
                .astype(BF16)
            )

    steps = groups // ROWS_STEP
    for step in range(steps // 2):
        mix(step)

    pl.semaphore_wait(barrier, peers - 1)
    asks = [
        pltpu.make_async_remote_copy(
            src_ref=asked.at[pl.ds(0, 2), :],
            dst_ref=asked.at[pl.ds(2 * offset, 2), :],
            send_sem=ask_send.at[offset],
            recv_sem=ask_recv.at[offset],
            device_id=device(offset),
            device_id_type=pl.DeviceIdType.MESH,
        )
        for offset in range(1, peers)
    ]
    for ask in asks:
        ask.start()
    for load in small[4:]:
        load.wait()
    for step in range(steps // 2, steps):
        mix(step)

    own = (iota((sub, order), 0) + me * sub == mode_labels[...]).astype(BF16)
    mode_real, mode_imag = dot(own, mode[0]), dot(own, mode[1])
    lane = iota((terms, span), 1)
    repeat = functools.reduce(
        jnp.logical_or,
        [lane == iota((terms, span), 0) + place * terms for place in range(TILE)],
    ).astype(BF16)
    blocks_of = jnp.concatenate(
        [
            dot(jnp.transpose(half).astype(BF16), repeat).reshape(row_blocks, fold, span)
            for half in complex_rows(mode_real, mode_imag, 0)
        ],
        1,
    )
    lane = iota(blocks_of.shape, 2)
    for place in range(TILE):
        inside = (lane >= place * terms) & (lane < (place + 1) * terms)
        coeffs[place] = jnp.where(inside, blocks_of, 0.0).astype(BF16)

    final_real = jnp.concatenate([final[0], final[1]], 1)
    final_imag = jnp.concatenate([-final[1], final[0]], 1)

    for ask in asks:
        ask.wait_recv()
    to_scalars = pltpu.make_async_copy(asked, indices, index_sem)
    to_scalars.start()
    to_scalars.wait()

    def products(first_slot, last_slot):
        first, last = first_slot * padded, last_slot * padded
        rows = last - first
        for start in range(first, last, TILE):
            left, right = [], []
            for place in range(TILE):
                slot, entry = (start + place) // padded, (start + place) % padded
                left.append(coeffs[place, indices[2 * slot + 1, entry]])
                right.append(spread[indices[2 * slot, entry]])
            partial[start * 2 * fold : (start + TILE) * 2 * fold, :] = dot(
                jnp.concatenate(left, 0), jnp.concatenate(right, 0)
            )
        pieces = [
            partial[pl.ds(first * 2 * fold + index, rows, stride=2 * fold), :].astype(BF16)
            for index in range(2 * fold)
        ]
        real = jnp.concatenate(pieces[:fold], 1)
        imag = jnp.concatenate(pieces[fold:], 1)
        return dot(real, final_real) + dot(imag, final_imag)

    gives = [
        pltpu.make_async_remote_copy(
            src_ref=outgoing.at[offset],
            dst_ref=incoming.at[offset],
            send_sem=give_send.at[offset],
            recv_sem=give_recv.at[offset],
            device_id=device(offset),
            device_id_type=pl.DeviceIdType.MESH,
        )
        for offset in range(1, peers)
    ]
    middle = peers // 2
    result = products(middle, peers)
    outgoing[middle:] = result.reshape(peers - middle, padded, 2 * out_width).astype(BF16)
    for give in gives[middle - 1 :]:
        give.start()
    result = products(0, middle)
    outgoing[:middle] = result.reshape(middle, padded, 2 * out_width).astype(BF16)
    for give in gives[: middle - 1]:
        give.start()
    answer = result[:padded]
    for offset in list(range(middle, peers)) + list(range(1, middle)):
        gives[offset - 1].wait_recv()
        answer = answer + incoming[offset].astype(F32)
    answer = answer.astype(out_ref.dtype)
    out_ref[0, 0] = answer[:count, :out_width]
    out_ref[1, 0] = answer[:count, out_width:]
    for copy in asks + gives:
        copy.wait_send()


def fused(mode_size, group_size, padded, arguments):
    stem_slice, column, row, mode, final, row_labels, mode_labels, requests = arguments
    peers = mode_size * group_size
    row_count, width = stem_slice.shape[2:]
    order = mode.shape[1]
    sub = order // peers
    fold = final.shape[1] // width
    out_width = final.shape[2]
    count = requests.shape[1]
    total = peers * padded
    terms = 2 * sub
    span = terms * TILE
    steps = row_count // row.shape[1] // ROWS_STEP
    row_labels = row_labels.reshape(1, -1)
    mode_labels = mode_labels.reshape(1, -1)
    dma = pltpu.SemaphoreType.DMA
    return pl.pallas_call(
        functools.partial(fused_kernel, mode_size, group_size),
        out_shape=pltpu.VMEM((2, 1, count, out_width), BF16),
        in_specs=[pl.BlockSpec(memory_space=pltpu.HBM)] * 8,
        out_specs=pl.BlockSpec(memory_space=pltpu.VMEM),
        scratch_shapes=[
            pltpu.VMEM((2, row_count, width), BF16),
            pltpu.VMEM(column.shape, BF16),
            pltpu.VMEM(row.shape, BF16),
            pltpu.VMEM(mode.shape, BF16),
            pltpu.VMEM(final.shape, BF16),
            pltpu.VMEM(row_labels.shape, jnp.int32),
            pltpu.VMEM(mode_labels.shape, jnp.int32),
            pltpu.VMEM(requests.shape, jnp.int32),
            pltpu.VMEM((2 * peers, width), jnp.int32),
            pltpu.SMEM((2 * peers, width), jnp.int32),
            pltpu.VMEM((row_count // sub, terms, width), BF16),
            pltpu.VMEM((TILE, order // fold, 2 * fold, span), BF16),
            pltpu.VMEM((total * 2 * fold, width), F32),
            pltpu.VMEM((peers, padded, 2 * out_width), BF16),
            pltpu.VMEM((peers, padded, 2 * out_width), BF16),
            dma((7,)),
            dma,
            dma((steps,)),
            dma((peers,)),
            dma((peers,)),
            dma((peers,)),
            dma((peers,)),
        ],
        compiler_params=pltpu.CompilerParams(
            collective_id=0, has_side_effects=True, vmem_limit_bytes=60 * 1024 * 1024
        ),
    )(stem_slice, column, row, mode, final, row_labels, mode_labels, requests)


def complex_table(weight):
    real_part = weight[0]
    imag_part = weight[1]
    return jnp.stack([jnp.stack([real_part, imag_part], 1), jnp.stack([-imag_part, real_part], 1)])


def relabel(weight, labels):
    label_count = labels.shape[0]
    onehot = (labels[:, None] == jnp.arange(label_count, dtype=jnp.int32)[None, :]).astype(
        jnp.float32
    )
    relabelled = jnp.einsum(
        "ji,zjn->zin", onehot, weight.astype(jnp.float32), precision=lax.Precision.HIGHEST
    )
    return complex_table(relabelled.astype(jnp.bfloat16))


def swapped(
    stem_slice,
    column_branch,
    row_branch,
    mode_branch,
    final_branch,
    row_labels,
    mode_labels,
    requests,
):
    local_block = stem_slice[:, 0]
    row_count = local_block.shape[1]
    col_width = local_block.shape[2]
    first_mixed = jnp.einsum(
        "zlc,zcwk->wlk",
        local_block,
        complex_table(column_branch),
        preferred_element_type=jnp.float32,
    ).astype(jnp.bfloat16)
    grouped = first_mixed.reshape(2, row_count // col_width, col_width, col_width)
    second = jnp.einsum(
        "zgjc,zjwk->wgkc",
        grouped,
        relabel(row_branch, row_labels),
        preferred_element_type=jnp.float32,
    ).astype(jnp.bfloat16)
    peer_count = lax.axis_size(("mode", "group"))
    order_size = mode_branch.shape[1]
    sub_rows = order_size // peer_count
    blocks = row_count // order_size
    mode_table = relabel(mode_branch, mode_labels).reshape(2, peer_count, sub_rows, 2, order_size)
    shaped = second.reshape(2, peer_count, blocks, sub_rows, col_width)
    mode_mixed = jnp.einsum(
        "zqhsc,zqswk->whkc",
        lax.all_to_all(shaped, ("mode", "group"), split_axis=1, concat_axis=1, tiled=True),
        mode_table,
        preferred_element_type=jnp.float32,
    ).astype(jnp.bfloat16)
    stem_rows = mode_mixed.reshape(2, row_count // 8, 8 * col_width)
    row_total = stem_rows.shape[1]
    wanted = requests[0]
    owner_index = wanted // row_total
    row_index = wanted - owner_index * row_total
    peer_ids = jnp.arange(peer_count, dtype=jnp.int32)
    onehot = (owner_index[:, None] == peer_ids[None, :]).astype(jnp.int32)
    slot_rank = jnp.sum((jnp.cumsum(onehot, axis=0) - onehot) * onehot, axis=1)
    flat_slot = owner_index * CAPACITY + slot_rank
    send_rows = (
        jnp.full((peer_count * CAPACITY,), -1, jnp.int32)
        .at[flat_slot]
        .set(row_index)
        .reshape(peer_count, CAPACITY)
    )
    asked_rows = lax.all_to_all(
        send_rows, ("mode", "group"), split_axis=0, concat_axis=0, tiled=True
    )
    safe_rows = jnp.maximum(asked_rows, 0).reshape(-1)
    final_table = complex_table(final_branch)
    results = jnp.einsum(
        "zlr,zrwk->wlk", stem_rows, final_table, preferred_element_type=jnp.float32
    ).astype(jnp.bfloat16)
    picked = jnp.take(results, safe_rows, axis=1).reshape(2, peer_count, CAPACITY, results.shape[2])
    returned = lax.all_to_all(picked, ("mode", "group"), split_axis=1, concat_axis=1, tiled=True)
    amplitudes = jnp.take(
        returned.reshape(2, peer_count * CAPACITY, results.shape[2]), flat_slot, axis=1
    )
    return amplitudes[:, None]


def per_device(mode_size, group_size, *arguments):
    stem_slice, _, row, mode, final, _, _, requests = arguments
    peers = mode_size * group_size
    row_count, width = stem_slice.shape[2:]
    padded = -(-requests.shape[1] // 16) * 16
    fits = (
        peers == TILE
        and padded <= width
        and row.shape[1] == width
        and mode.shape[1] % (16 * peers) == 0
        and row_count % (ROWS_STEP * width) == 0
        and 2 * peers * padded * final.shape[2] < stem_slice.size
    )
    if fits:
        return fused(mode_size, group_size, padded, arguments)
    return swapped(*arguments)


def solution(mesh):
    return jax.shard_map(
        functools.partial(per_device, mesh.shape["mode"], mesh.shape["group"]),
        mesh=mesh,
        in_specs=(
            P(None, ("cuts", "batch"), ("mode", "group"), None),
            P(),
            P(),
            P(),
            P(),
            P(),
            P(),
            P("batch", ("mode", "group")),
        ),
        out_specs=P(None, ("cuts", "batch"), ("mode", "group"), None),
        check_vma=False,
    )
```

```python
import functools

import jax
import jax.numpy as jnp
from jax import lax
from jax.experimental import pallas as pl
from jax.experimental.pallas import tpu as pltpu
from jax.sharding import PartitionSpec as P

CAPACITY = 8
TILE = 8
CHUNK_SLOTS = 2
ROWS_STEP = 2

F32 = jnp.float32
BF16 = jnp.bfloat16


def dot(left, right):
    return jnp.dot(left, right, preferred_element_type=F32)


def dot_t(left, right):
    return lax.dot_general(left, right, (((0,), (1,)), ((), ())), preferred_element_type=F32)


def iota(shape, dim):
    return lax.broadcasted_iota(jnp.int32, shape, dim)


def complex_rows(real, imag, axis):
    return jnp.concatenate([real, -imag], axis), jnp.concatenate([imag, real], axis)


def fused_kernel(
    mode_size,
    group_size,
    stem_hbm,
    column_hbm,
    row_hbm,
    mode_hbm,
    final_hbm,
    row_labels_hbm,
    mode_labels_hbm,
    requests_hbm,
    out_ref,
    stem,
    column,
    row,
    mode,
    final,
    row_labels,
    mode_labels,
    wanted,
    asked,
    indices,
    spread,
    coeffs,
    partial,
    outgoing,
    incoming,
    load_sem,
    index_sem,
    stem_sem,
    ask_send,
    ask_recv,
    give_send,
    give_recv,
):
    peers = mode_size * group_size
    row_count, width = stem.shape[1], stem.shape[2]
    row_order = row.shape[1]
    order = mode.shape[1]
    sub = order // peers
    heads = row_order // sub
    groups = row_count // row_order
    length = final.shape[1]
    fold = length // width
    out_width = final.shape[2]
    count = wanted.shape[1]
    padded = outgoing.shape[1]
    blocks = row_count // sub
    row_blocks = order // fold
    terms = 2 * sub
    span = terms * TILE

    mode_index = lax.axis_index("mode")
    group_index = lax.axis_index("group")
    me = mode_index * group_size + group_index

    def device(offset):
        peer = me
        bit = 1
        while bit <= offset:
            if offset & bit:
                peer = peer + bit - 2 * bit * lax.rem(peer // bit, 2)
            bit *= 2
        return {"mode": peer // group_size, "group": lax.rem(peer, group_size)}

    barrier = pltpu.get_barrier_semaphore()
    for offset in range(1, peers):
        pl.semaphore_signal(
            barrier, inc=1, device_id=device(offset), device_id_type=pl.DeviceIdType.MESH
        )

    small = [
        pltpu.make_async_copy(source, target, load_sem.at[index])
        for index, (source, target) in enumerate(
            (
                (requests_hbm, wanted),
                (column_hbm, column),
                (row_hbm, row),
                (row_labels_hbm, row_labels),
                (mode_hbm, mode),
                (mode_labels_hbm, mode_labels),
                (final_hbm, final),
            )
        )
    ]
    step_rows = ROWS_STEP * row_order
    stem_loads = [
        pltpu.make_async_copy(
            stem_hbm.at[:, 0, pl.ds(step * step_rows, step_rows), :],
            stem.at[:, pl.ds(step * step_rows, step_rows), :],
            stem_sem.at[step],
        )
        for step in range(groups // ROWS_STEP)
    ]
    for load in small[:4] + stem_loads + small[4:]:
        load.start()

    small[0].wait()
    asked[0:2, :] = jnp.zeros((2, width), jnp.int32)
    asked[0:1, 0:count] = lax.div(wanted[...], row_blocks)
    asked[1:2, 0:count] = lax.rem(wanted[...], row_blocks)
    for load in small[1:4]:
        load.wait()

    column_real, column_imag = complex_rows(column[0], column[1], 0)
    column_table = jnp.concatenate([column_real, column_imag], 1)
    chosen = (iota((row_order, row_order), 0) == row_labels[...]).astype(BF16)

    def relabelled(weight):
        return dot_t(weight, chosen).astype(BF16)

    row_table = jnp.concatenate(
        [
            half.reshape(heads, sub, 2 * row_order)
            for half in complex_rows(relabelled(row[0]), relabelled(row[1]), 1)
        ],
        1,
    ).reshape(2 * row_order, 2 * row_order)

    pl.semaphore_wait(barrier, peers - 1)
    asks = [
        pltpu.make_async_remote_copy(
            src_ref=asked.at[pl.ds(0, 2), :],
            dst_ref=asked.at[pl.ds(2 * offset, 2), :],
            send_sem=ask_send.at[offset],
            recv_sem=ask_recv.at[offset],
            device_id=device(offset),
            device_id_type=pl.DeviceIdType.MESH,
        )
        for offset in range(1, peers)
    ]
    for ask in asks:
        ask.start()
    for load in stem_loads + small[4:]:
        load.wait()

    def mix(step):
        rows = pl.ds(step * step_rows, step_rows)
        operand = jnp.concatenate([stem[0, rows, :], stem[1, rows, :]], 1)
        mixed = dot(operand, column_table).astype(BF16)
        pieces = []
        for index in range(ROWS_STEP):
            piece = mixed[index * row_order : (index + 1) * row_order]
            pieces.append(jnp.concatenate([piece[:, :width], piece[:, width:]], 0))
        result = dot(row_table, jnp.concatenate(pieces, 1))
        for index in range(ROWS_STEP):
            first = (step * ROWS_STEP + index) * heads
            spread[first : first + heads] = (
                result[:, index * width : (index + 1) * width]
                .reshape(heads, terms, width)
                .astype(BF16)
            )

    for step in range(groups // ROWS_STEP):
        mix(step)

    own = (iota((sub, order), 0) + me * sub == mode_labels[...]).astype(BF16)
    mode_real, mode_imag = dot(own, mode[0]), dot(own, mode[1])
    lane = iota((terms, span), 1)
    repeat = functools.reduce(
        jnp.logical_or,
        [lane == iota((terms, span), 0) + place * terms for place in range(TILE)],
    ).astype(BF16)
    blocks_of = jnp.concatenate(
        [
            dot(jnp.transpose(half).astype(BF16), repeat).reshape(row_blocks, fold, span)
            for half in complex_rows(mode_real, mode_imag, 0)
        ],
        1,
    )
    lane = iota(blocks_of.shape, 2)
    for place in range(TILE):
        inside = (lane >= place * terms) & (lane < (place + 1) * terms)
        coeffs[place] = jnp.where(inside, blocks_of, 0.0).astype(BF16)

    final_real = jnp.concatenate([final[0], final[1]], 1)
    final_imag = jnp.concatenate([-final[1], final[0]], 1)

    def bring(chunk):
        first_slot = chunk * CHUNK_SLOTS
        for slot in range(max(first_slot, 1), first_slot + CHUNK_SLOTS):
            asks[slot - 1].wait_recv()
        rows = pl.ds(2 * first_slot, 2 * CHUNK_SLOTS)
        copy = pltpu.make_async_copy(asked.at[rows, :], indices.at[rows, :], index_sem.at[chunk])
        copy.start()
        return copy

    def products(first_slot, last_slot):
        first, last = first_slot * padded, last_slot * padded
        rows = last - first
        for start in range(first, last, TILE):
            left, right = [], []
            for place in range(TILE):
                slot, entry = (start + place) // padded, (start + place) % padded
                left.append(coeffs[place, indices[2 * slot + 1, entry]])
                right.append(spread[indices[2 * slot, entry]])
            partial[start * 2 * fold : (start + TILE) * 2 * fold, :] = dot(
                jnp.concatenate(left, 0), jnp.concatenate(right, 0)
            )
        pieces = [
            partial[pl.ds(first * 2 * fold + index, rows, stride=2 * fold), :].astype(BF16)
            for index in range(2 * fold)
        ]
        real = jnp.concatenate(pieces[:fold], 1)
        imag = jnp.concatenate(pieces[fold:], 1)
        return dot(real, final_real) + dot(imag, final_imag)

    gives = [
        pltpu.make_async_remote_copy(
            src_ref=outgoing.at[offset],
            dst_ref=incoming.at[offset],
            send_sem=give_send.at[offset],
            recv_sem=give_recv.at[offset],
            device_id=device(offset),
            device_id_type=pl.DeviceIdType.MESH,
        )
        for offset in range(1, peers)
    ]
    chunks = peers // CHUNK_SLOTS
    ready = bring(chunks - 1)
    for chunk in reversed(range(chunks)):
        ready.wait()
        if chunk:
            ready = bring(chunk - 1)
        first = chunk * CHUNK_SLOTS
        last = first + CHUNK_SLOTS
        result = products(first, last)
        outgoing[first:last] = result.reshape(CHUNK_SLOTS, padded, 2 * out_width).astype(BF16)
        for give in gives[max(first, 1) - 1 : last - 1]:
            give.start()
    answer = result[:padded]
    for offset in reversed(range(1, peers)):
        gives[offset - 1].wait_recv()
        answer = answer + incoming[offset].astype(F32)
    answer = answer.astype(out_ref.dtype)
    out_ref[0, 0] = answer[:count, :out_width]
    out_ref[1, 0] = answer[:count, out_width:]
    for copy in asks + gives:
        copy.wait_send()


def fused(mode_size, group_size, padded, arguments):
    stem_slice, column, row, mode, final, row_labels, mode_labels, requests = arguments
    peers = mode_size * group_size
    row_count, width = stem_slice.shape[2:]
    order = mode.shape[1]
    sub = order // peers
    fold = final.shape[1] // width
    out_width = final.shape[2]
    count = requests.shape[1]
    total = peers * padded
    terms = 2 * sub
    span = terms * TILE
    steps = row_count // row.shape[1] // ROWS_STEP
    row_labels = row_labels.reshape(1, -1)
    mode_labels = mode_labels.reshape(1, -1)
    dma = pltpu.SemaphoreType.DMA
    return pl.pallas_call(
        functools.partial(fused_kernel, mode_size, group_size),
        out_shape=pltpu.VMEM((2, 1, count, out_width), BF16),
        in_specs=[pl.BlockSpec(memory_space=pltpu.HBM)] * 8,
        out_specs=pl.BlockSpec(memory_space=pltpu.VMEM),
        scratch_shapes=[
            pltpu.VMEM((2, row_count, width), BF16),
            pltpu.VMEM(column.shape, BF16),
            pltpu.VMEM(row.shape, BF16),
            pltpu.VMEM(mode.shape, BF16),
            pltpu.VMEM(final.shape, BF16),
            pltpu.VMEM(row_labels.shape, jnp.int32),
            pltpu.VMEM(mode_labels.shape, jnp.int32),
            pltpu.VMEM(requests.shape, jnp.int32),
            pltpu.VMEM((2 * peers, width), jnp.int32),
            pltpu.SMEM((2 * peers, width), jnp.int32),
            pltpu.VMEM((row_count // sub, terms, width), BF16),
            pltpu.VMEM((TILE, order // fold, 2 * fold, span), BF16),
            pltpu.VMEM((total * 2 * fold, width), F32),
            pltpu.VMEM((peers, padded, 2 * out_width), BF16),
            pltpu.VMEM((peers, padded, 2 * out_width), BF16),
            dma((7,)),
            dma((peers // CHUNK_SLOTS,)),
            dma((steps,)),
            dma((peers,)),
            dma((peers,)),
            dma((peers,)),
            dma((peers,)),
        ],
        compiler_params=pltpu.CompilerParams(
            collective_id=0, has_side_effects=True, vmem_limit_bytes=60 * 1024 * 1024
        ),
    )(stem_slice, column, row, mode, final, row_labels, mode_labels, requests)


def complex_table(weight):
    real_part = weight[0]
    imag_part = weight[1]
    return jnp.stack([jnp.stack([real_part, imag_part], 1), jnp.stack([-imag_part, real_part], 1)])


def relabel(weight, labels):
    label_count = labels.shape[0]
    onehot = (labels[:, None] == jnp.arange(label_count, dtype=jnp.int32)[None, :]).astype(
        jnp.float32
    )
    relabelled = jnp.einsum(
        "ji,zjn->zin", onehot, weight.astype(jnp.float32), precision=lax.Precision.HIGHEST
    )
    return complex_table(relabelled.astype(jnp.bfloat16))


def swapped(
    stem_slice,
    column_branch,
    row_branch,
    mode_branch,
    final_branch,
    row_labels,
    mode_labels,
    requests,
):
    local_block = stem_slice[:, 0]
    row_count = local_block.shape[1]
    col_width = local_block.shape[2]
    first_mixed = jnp.einsum(
        "zlc,zcwk->wlk",
        local_block,
        complex_table(column_branch),
        preferred_element_type=jnp.float32,
    ).astype(jnp.bfloat16)
    grouped = first_mixed.reshape(2, row_count // col_width, col_width, col_width)
    second = jnp.einsum(
        "zgjc,zjwk->wgkc",
        grouped,
        relabel(row_branch, row_labels),
        preferred_element_type=jnp.float32,
    ).astype(jnp.bfloat16)
    peer_count = lax.axis_size(("mode", "group"))
    order_size = mode_branch.shape[1]
    sub_rows = order_size // peer_count
    blocks = row_count // order_size
    mode_table = relabel(mode_branch, mode_labels).reshape(2, peer_count, sub_rows, 2, order_size)
    shaped = second.reshape(2, peer_count, blocks, sub_rows, col_width)
    mode_mixed = jnp.einsum(
        "zqhsc,zqswk->whkc",
        lax.all_to_all(shaped, ("mode", "group"), split_axis=1, concat_axis=1, tiled=True),
        mode_table,
        preferred_element_type=jnp.float32,
    ).astype(jnp.bfloat16)
    stem_rows = mode_mixed.reshape(2, row_count // 8, 8 * col_width)
    row_total = stem_rows.shape[1]
    wanted = requests[0]
    owner_index = wanted // row_total
    row_index = wanted - owner_index * row_total
    peer_ids = jnp.arange(peer_count, dtype=jnp.int32)
    onehot = (owner_index[:, None] == peer_ids[None, :]).astype(jnp.int32)
    slot_rank = jnp.sum((jnp.cumsum(onehot, axis=0) - onehot) * onehot, axis=1)
    flat_slot = owner_index * CAPACITY + slot_rank
    send_rows = (
        jnp.full((peer_count * CAPACITY,), -1, jnp.int32)
        .at[flat_slot]
        .set(row_index)
        .reshape(peer_count, CAPACITY)
    )
    asked_rows = lax.all_to_all(
        send_rows, ("mode", "group"), split_axis=0, concat_axis=0, tiled=True
    )
    safe_rows = jnp.maximum(asked_rows, 0).reshape(-1)
    final_table = complex_table(final_branch)
    results = jnp.einsum(
        "zlr,zrwk->wlk", stem_rows, final_table, preferred_element_type=jnp.float32
    ).astype(jnp.bfloat16)
    picked = jnp.take(results, safe_rows, axis=1).reshape(2, peer_count, CAPACITY, results.shape[2])
    returned = lax.all_to_all(picked, ("mode", "group"), split_axis=1, concat_axis=1, tiled=True)
    amplitudes = jnp.take(
        returned.reshape(2, peer_count * CAPACITY, results.shape[2]), flat_slot, axis=1
    )
    return amplitudes[:, None]


def per_device(mode_size, group_size, *arguments):
    stem_slice, _, row, mode, final, _, _, requests = arguments
    peers = mode_size * group_size
    row_count, width = stem_slice.shape[2:]
    padded = -(-requests.shape[1] // 16) * 16
    fits = (
        peers == TILE
        and padded <= width
        and row.shape[1] == width
        and mode.shape[1] % (16 * peers) == 0
        and row_count % (ROWS_STEP * width) == 0
        and 2 * peers * padded * final.shape[2] < stem_slice.size
    )
    if fits:
        return fused(mode_size, group_size, padded, arguments)
    return swapped(*arguments)


def solution(mesh):
    return jax.shard_map(
        functools.partial(per_device, mesh.shape["mode"], mesh.shape["group"]),
        mesh=mesh,
        in_specs=(
            P(None, ("cuts", "batch"), ("mode", "group"), None),
            P(),
            P(),
            P(),
            P(),
            P(),
            P(),
            P("batch", ("mode", "group")),
        ),
        out_specs=P(None, ("cuts", "batch"), ("mode", "group"), None),
        check_vma=False,
    )
```

```python
import functools

import jax
import jax.numpy as jnp
from jax import lax
from jax.experimental import pallas as pl
from jax.experimental.pallas import tpu as pltpu
from jax.sharding import PartitionSpec as P

CAPACITY = 8
TILE = 8
ROWS_STEP = 2

F32 = jnp.float32
BF16 = jnp.bfloat16


def dot(left, right):
    return jnp.dot(left, right, preferred_element_type=F32)


def dot_t(left, right):
    return lax.dot_general(left, right, (((0,), (1,)), ((), ())), preferred_element_type=F32)


def iota(shape, dim):
    return lax.broadcasted_iota(jnp.int32, shape, dim)


def complex_rows(real, imag, axis):
    return jnp.concatenate([real, -imag], axis), jnp.concatenate([imag, real], axis)


def fused_kernel(
    mode_size,
    group_size,
    stem_hbm,
    column_hbm,
    row_hbm,
    mode_hbm,
    final_hbm,
    row_labels_hbm,
    mode_labels_hbm,
    requests_hbm,
    out_ref,
    stem,
    column,
    row,
    mode,
    final,
    row_labels,
    mode_labels,
    wanted,
    asked,
    indices,
    spread,
    coeffs,
    partial,
    outgoing,
    incoming,
    load_sem,
    index_sem,
    stem_sem,
    ask_send,
    ask_recv,
    give_send,
    give_recv,
):
    peers = mode_size * group_size
    row_count, width = stem.shape[1], stem.shape[2]
    row_order = row.shape[1]
    order = mode.shape[1]
    sub = order // peers
    heads = row_order // sub
    groups = row_count // row_order
    length = final.shape[1]
    fold = length // width
    out_width = final.shape[2]
    count = wanted.shape[1]
    padded = outgoing.shape[1]
    blocks = row_count // sub
    row_blocks = order // fold
    terms = 2 * sub
    span = terms * TILE

    mode_index = lax.axis_index("mode")
    group_index = lax.axis_index("group")
    me = mode_index * group_size + group_index

    def device(offset):
        peer = me
        bit = 1
        while bit <= offset:
            if offset & bit:
                peer = peer + bit - 2 * bit * lax.rem(peer // bit, 2)
            bit *= 2
        return {"mode": peer // group_size, "group": lax.rem(peer, group_size)}

    barrier = pltpu.get_barrier_semaphore()
    for offset in range(1, peers):
        pl.semaphore_signal(
            barrier, inc=1, device_id=device(offset), device_id_type=pl.DeviceIdType.MESH
        )

    small = [
        pltpu.make_async_copy(source, target, load_sem.at[index])
        for index, (source, target) in enumerate(
            (
                (requests_hbm, wanted),
                (column_hbm, column),
                (row_hbm, row),
                (row_labels_hbm, row_labels),
                (mode_hbm, mode),
                (mode_labels_hbm, mode_labels),
                (final_hbm, final),
            )
        )
    ]
    step_rows = ROWS_STEP * row_order
    stem_loads = [
        pltpu.make_async_copy(
            stem_hbm.at[half, 0], stem.at[half], stem_sem.at[half]
        )
        for half in range(2)
    ]
    for load in small[:4] + stem_loads + small[4:]:
        load.start()

    small[0].wait()
    asked[0:2, :] = jnp.zeros((2, width), jnp.int32)
    asked[0:1, 0:count] = lax.div(wanted[...], row_blocks)
    asked[1:2, 0:count] = lax.rem(wanted[...], row_blocks)
    for load in small[1:4]:
        load.wait()

    column_real, column_imag = complex_rows(column[0], column[1], 0)
    column_table = jnp.concatenate([column_real, column_imag], 1)
    chosen = (iota((row_order, row_order), 0) == row_labels[...]).astype(BF16)

    def relabelled(weight):
        return dot_t(weight, chosen).astype(BF16)

    row_table = jnp.concatenate(
        [
            half.reshape(heads, sub, 2 * row_order)
            for half in complex_rows(relabelled(row[0]), relabelled(row[1]), 1)
        ],
        1,
    ).reshape(2 * row_order, 2 * row_order)

    pl.semaphore_wait(barrier, peers - 1)
    asks = [
        pltpu.make_async_remote_copy(
            src_ref=asked.at[pl.ds(0, 2), :],
            dst_ref=asked.at[pl.ds(2 * offset, 2), :],
            send_sem=ask_send.at[offset],
            recv_sem=ask_recv.at[offset],
            device_id=device(offset),
            device_id_type=pl.DeviceIdType.MESH,
        )
        for offset in range(1, peers)
    ]
    for ask in asks:
        ask.start()
    for load in stem_loads + small[4:]:
        load.wait()

    def mix(step):
        rows = pl.ds(step * step_rows, step_rows)
        operand = jnp.concatenate([stem[0, rows, :], stem[1, rows, :]], 1)
        mixed = dot(operand, column_table).astype(BF16)
        pieces = []
        for index in range(ROWS_STEP):
            piece = mixed[index * row_order : (index + 1) * row_order]
            pieces.append(jnp.concatenate([piece[:, :width], piece[:, width:]], 0))
        result = dot(row_table, jnp.concatenate(pieces, 1))
        for index in range(ROWS_STEP):
            first = (step * ROWS_STEP + index) * heads
            spread[first : first + heads] = (
                result[:, index * width : (index + 1) * width]
                .reshape(heads, terms, width)
                .astype(BF16)
            )

    for step in range(groups // ROWS_STEP):
        mix(step)

    own = (iota((sub, order), 0) + me * sub == mode_labels[...]).astype(BF16)
    mode_real, mode_imag = dot(own, mode[0]), dot(own, mode[1])
    lane = iota((terms, span), 1)
    repeat = functools.reduce(
        jnp.logical_or,
        [lane == iota((terms, span), 0) + place * terms for place in range(TILE)],
    ).astype(BF16)
    blocks_of = jnp.concatenate(
        [
            dot(jnp.transpose(half).astype(BF16), repeat).reshape(row_blocks, fold, span)
            for half in complex_rows(mode_real, mode_imag, 0)
        ],
        1,
    )
    lane = iota(blocks_of.shape, 2)
    for place in range(TILE):
        inside = (lane >= place * terms) & (lane < (place + 1) * terms)
        coeffs[place] = jnp.where(inside, blocks_of, 0.0).astype(BF16)

    final_real = jnp.concatenate([final[0], final[1]], 1)
    final_imag = jnp.concatenate([-final[1], final[0]], 1)

    for ask in asks:
        ask.wait_recv()
    to_scalars = pltpu.make_async_copy(asked, indices, index_sem)
    to_scalars.start()
    to_scalars.wait()

    def mode_products(first_slot, last_slot):
        first, last = first_slot * padded, last_slot * padded
        for start in range(first, last, TILE):
            left, right = [], []
            for place in range(TILE):
                slot, entry = (start + place) // padded, (start + place) % padded
                left.append(coeffs[place, indices[2 * slot + 1, entry]])
                right.append(spread[indices[2 * slot, entry]])
            partial[start * 2 * fold : (start + TILE) * 2 * fold, :] = dot(
                jnp.concatenate(left, 0), jnp.concatenate(right, 0)
            )

    def final_products(first_slot, last_slot):
        first, rows = first_slot * padded, (last_slot - first_slot) * padded
        pieces = [
            partial[pl.ds(first * 2 * fold + index, rows, stride=2 * fold), :].astype(BF16)
            for index in range(2 * fold)
        ]
        real = jnp.concatenate(pieces[:fold], 1)
        imag = jnp.concatenate(pieces[fold:], 1)
        return dot(real, final_real) + dot(imag, final_imag)

    gives = [
        pltpu.make_async_remote_copy(
            src_ref=outgoing.at[offset],
            dst_ref=incoming.at[offset],
            send_sem=give_send.at[offset],
            recv_sem=give_recv.at[offset],
            device_id=device(offset),
            device_id_type=pl.DeviceIdType.MESH,
        )
        for offset in range(1, peers)
    ]
    middle = peers // 2
    edges = [peers, middle + middle // 2, middle, 1, 0]
    chunks = list(zip(edges[1:], edges[:-1]))
    mode_products(*chunks[0])
    for index, (first, last) in enumerate(chunks):
        if index + 1 < len(chunks):
            mode_products(*chunks[index + 1])
        result = final_products(first, last)
        if first:
            outgoing[first:last] = result.reshape(last - first, padded, 2 * out_width).astype(BF16)
            for give in gives[first - 1 : last - 1]:
                give.start()
    answer = result
    for offset in reversed(range(1, peers)):
        gives[offset - 1].wait_recv()
        answer = answer + incoming[offset].astype(F32)
    answer = answer.astype(out_ref.dtype)
    out_ref[0, 0] = answer[:count, :out_width]
    out_ref[1, 0] = answer[:count, out_width:]
    for copy in asks + gives:
        copy.wait_send()


def fused(mode_size, group_size, padded, arguments):
    stem_slice, column, row, mode, final, row_labels, mode_labels, requests = arguments
    peers = mode_size * group_size
    row_count, width = stem_slice.shape[2:]
    order = mode.shape[1]
    sub = order // peers
    fold = final.shape[1] // width
    out_width = final.shape[2]
    count = requests.shape[1]
    total = peers * padded
    terms = 2 * sub
    span = terms * TILE
    row_labels = row_labels.reshape(1, -1)
    mode_labels = mode_labels.reshape(1, -1)
    dma = pltpu.SemaphoreType.DMA
    return pl.pallas_call(
        functools.partial(fused_kernel, mode_size, group_size),
        out_shape=pltpu.VMEM((2, 1, count, out_width), BF16),
        in_specs=[pl.BlockSpec(memory_space=pltpu.HBM)] * 8,
        out_specs=pl.BlockSpec(memory_space=pltpu.VMEM),
        scratch_shapes=[
            pltpu.VMEM((2, row_count, width), BF16),
            pltpu.VMEM(column.shape, BF16),
            pltpu.VMEM(row.shape, BF16),
            pltpu.VMEM(mode.shape, BF16),
            pltpu.VMEM(final.shape, BF16),
            pltpu.VMEM(row_labels.shape, jnp.int32),
            pltpu.VMEM(mode_labels.shape, jnp.int32),
            pltpu.VMEM(requests.shape, jnp.int32),
            pltpu.VMEM((2 * peers, width), jnp.int32),
            pltpu.SMEM((2 * peers, width), jnp.int32),
            pltpu.VMEM((row_count // sub, terms, width), BF16),
            pltpu.VMEM((TILE, order // fold, 2 * fold, span), BF16),
            pltpu.VMEM((total * 2 * fold, width), F32),
            pltpu.VMEM((peers, padded, 2 * out_width), BF16),
            pltpu.VMEM((peers, padded, 2 * out_width), BF16),
            dma((7,)),
            dma,
            dma((2,)),
            dma((peers,)),
            dma((peers,)),
            dma((peers,)),
            dma((peers,)),
        ],
        compiler_params=pltpu.CompilerParams(
            collective_id=0, has_side_effects=True, vmem_limit_bytes=60 * 1024 * 1024
        ),
    )(stem_slice, column, row, mode, final, row_labels, mode_labels, requests)


def complex_table(weight):
    real_part = weight[0]
    imag_part = weight[1]
    return jnp.stack([jnp.stack([real_part, imag_part], 1), jnp.stack([-imag_part, real_part], 1)])


def relabel(weight, labels):
    label_count = labels.shape[0]
    onehot = (labels[:, None] == jnp.arange(label_count, dtype=jnp.int32)[None, :]).astype(
        jnp.float32
    )
    relabelled = jnp.einsum(
        "ji,zjn->zin", onehot, weight.astype(jnp.float32), precision=lax.Precision.HIGHEST
    )
    return complex_table(relabelled.astype(jnp.bfloat16))


def swapped(
    stem_slice,
    column_branch,
    row_branch,
    mode_branch,
    final_branch,
    row_labels,
    mode_labels,
    requests,
):
    local_block = stem_slice[:, 0]
    row_count = local_block.shape[1]
    col_width = local_block.shape[2]
    first_mixed = jnp.einsum(
        "zlc,zcwk->wlk",
        local_block,
        complex_table(column_branch),
        preferred_element_type=jnp.float32,
    ).astype(jnp.bfloat16)
    grouped = first_mixed.reshape(2, row_count // col_width, col_width, col_width)
    second = jnp.einsum(
        "zgjc,zjwk->wgkc",
        grouped,
        relabel(row_branch, row_labels),
        preferred_element_type=jnp.float32,
    ).astype(jnp.bfloat16)
    peer_count = lax.axis_size(("mode", "group"))
    order_size = mode_branch.shape[1]
    sub_rows = order_size // peer_count
    blocks = row_count // order_size
    mode_table = relabel(mode_branch, mode_labels).reshape(2, peer_count, sub_rows, 2, order_size)
    shaped = second.reshape(2, peer_count, blocks, sub_rows, col_width)
    mode_mixed = jnp.einsum(
        "zqhsc,zqswk->whkc",
        lax.all_to_all(shaped, ("mode", "group"), split_axis=1, concat_axis=1, tiled=True),
        mode_table,
        preferred_element_type=jnp.float32,
    ).astype(jnp.bfloat16)
    stem_rows = mode_mixed.reshape(2, row_count // 8, 8 * col_width)
    row_total = stem_rows.shape[1]
    wanted = requests[0]
    owner_index = wanted // row_total
    row_index = wanted - owner_index * row_total
    peer_ids = jnp.arange(peer_count, dtype=jnp.int32)
    onehot = (owner_index[:, None] == peer_ids[None, :]).astype(jnp.int32)
    slot_rank = jnp.sum((jnp.cumsum(onehot, axis=0) - onehot) * onehot, axis=1)
    flat_slot = owner_index * CAPACITY + slot_rank
    send_rows = (
        jnp.full((peer_count * CAPACITY,), -1, jnp.int32)
        .at[flat_slot]
        .set(row_index)
        .reshape(peer_count, CAPACITY)
    )
    asked_rows = lax.all_to_all(
        send_rows, ("mode", "group"), split_axis=0, concat_axis=0, tiled=True
    )
    safe_rows = jnp.maximum(asked_rows, 0).reshape(-1)
    final_table = complex_table(final_branch)
    results = jnp.einsum(
        "zlr,zrwk->wlk", stem_rows, final_table, preferred_element_type=jnp.float32
    ).astype(jnp.bfloat16)
    picked = jnp.take(results, safe_rows, axis=1).reshape(2, peer_count, CAPACITY, results.shape[2])
    returned = lax.all_to_all(picked, ("mode", "group"), split_axis=1, concat_axis=1, tiled=True)
    amplitudes = jnp.take(
        returned.reshape(2, peer_count * CAPACITY, results.shape[2]), flat_slot, axis=1
    )
    return amplitudes[:, None]


def per_device(mode_size, group_size, *arguments):
    stem_slice, _, row, mode, final, _, _, requests = arguments
    peers = mode_size * group_size
    row_count, width = stem_slice.shape[2:]
    padded = -(-requests.shape[1] // 16) * 16
    fits = (
        peers == TILE
        and padded <= width
        and row.shape[1] == width
        and mode.shape[1] % (16 * peers) == 0
        and row_count % (ROWS_STEP * width) == 0
        and 2 * peers * padded * final.shape[2] < stem_slice.size
    )
    if fits:
        return fused(mode_size, group_size, padded, arguments)
    return swapped(*arguments)


def solution(mesh):
    return jax.shard_map(
        functools.partial(per_device, mesh.shape["mode"], mesh.shape["group"]),
        mesh=mesh,
        in_specs=(
            P(None, ("cuts", "batch"), ("mode", "group"), None),
            P(),
            P(),
            P(),
            P(),
            P(),
            P(),
            P("batch", ("mode", "group")),
        ),
        out_specs=P(None, ("cuts", "batch"), ("mode", "group"), None),
        check_vma=False,
    )
```

```python
import functools

import jax
import jax.numpy as jnp
from jax import lax
from jax.experimental import pallas as pl
from jax.experimental.pallas import tpu as pltpu
from jax.sharding import PartitionSpec as P

CAPACITY = 8
TILE = 8
ROWS_STEP = 2

F32 = jnp.float32
BF16 = jnp.bfloat16


def dot(left, right):
    return jnp.dot(left, right, preferred_element_type=F32)


def dot_t(left, right):
    return lax.dot_general(left, right, (((0,), (1,)), ((), ())), preferred_element_type=F32)


def iota(shape, dim):
    return lax.broadcasted_iota(jnp.int32, shape, dim)


def complex_rows(real, imag, axis):
    return jnp.concatenate([real, -imag], axis), jnp.concatenate([imag, real], axis)


def fused_kernel(
    mode_size,
    group_size,
    stem_hbm,
    column_hbm,
    row_hbm,
    mode_hbm,
    final_hbm,
    row_labels_hbm,
    mode_labels_hbm,
    requests_hbm,
    out_ref,
    stem,
    column,
    row,
    mode,
    final,
    row_labels,
    mode_labels,
    wanted,
    asked,
    indices,
    spread,
    coeffs,
    final_table,
    partial,
    outgoing,
    incoming,
    load_sem,
    index_sem,
    stem_sem,
    ask_send,
    ask_recv,
    give_send,
    give_recv,
):
    peers = mode_size * group_size
    row_count, width = stem.shape[1], stem.shape[2]
    row_order = row.shape[1]
    order = mode.shape[1]
    sub = order // peers
    heads = row_order // sub
    groups = row_count // row_order
    length = final.shape[1]
    fold = length // width
    out_width = final.shape[2]
    count = wanted.shape[1]
    padded = outgoing.shape[1]
    blocks = row_count // sub
    row_blocks = order // fold
    terms = 2 * sub
    span = terms * TILE

    mode_index = lax.axis_index("mode")
    group_index = lax.axis_index("group")
    me = mode_index * group_size + group_index

    def device(offset):
        peer = me
        bit = 1
        while bit <= offset:
            if offset & bit:
                peer = peer + bit - 2 * bit * lax.rem(peer // bit, 2)
            bit *= 2
        return {"mode": peer // group_size, "group": lax.rem(peer, group_size)}

    barrier = pltpu.get_barrier_semaphore()
    for offset in range(1, peers):
        pl.semaphore_signal(
            barrier, inc=1, device_id=device(offset), device_id_type=pl.DeviceIdType.MESH
        )

    small = [
        pltpu.make_async_copy(source, target, load_sem.at[index])
        for index, (source, target) in enumerate(
            (
                (requests_hbm, wanted),
                (column_hbm, column),
                (row_hbm, row),
                (row_labels_hbm, row_labels),
                (mode_hbm, mode),
                (mode_labels_hbm, mode_labels),
                (final_hbm, final),
            )
        )
    ]
    step_rows = ROWS_STEP * row_order
    stem_loads = [
        pltpu.make_async_copy(stem_hbm.at[half, 0], stem.at[half], stem_sem.at[half])
        for half in range(2)
    ]
    for load in small[:4] + stem_loads + small[4:]:
        load.start()

    small[0].wait()
    asked[0:2, :] = jnp.zeros((2, width), jnp.int32)
    asked[0:1, 0:count] = lax.div(wanted[...], row_blocks)
    asked[1:2, 0:count] = lax.rem(wanted[...], row_blocks)
    for load in small[1:4]:
        load.wait()

    column_real, column_imag = complex_rows(column[0], column[1], 0)
    column_table = jnp.concatenate([column_real, column_imag], 1)
    chosen = (iota((row_order, row_order), 0) == row_labels[...]).astype(BF16)

    def relabelled(weight):
        return dot_t(weight, chosen).astype(BF16)

    row_table = jnp.concatenate(
        [
            half.reshape(heads, sub, 2 * row_order)
            for half in complex_rows(relabelled(row[0]), relabelled(row[1]), 1)
        ],
        1,
    ).reshape(2 * row_order, 2 * row_order)

    pl.semaphore_wait(barrier, peers - 1)
    asks = [
        pltpu.make_async_remote_copy(
            src_ref=asked.at[pl.ds(0, 2), :],
            dst_ref=asked.at[pl.ds(2 * offset, 2), :],
            send_sem=ask_send.at[offset],
            recv_sem=ask_recv.at[offset],
            device_id=device(offset),
            device_id_type=pl.DeviceIdType.MESH,
        )
        for offset in range(1, peers)
    ]
    for ask in asks:
        ask.start()
    for load in stem_loads + small[4:]:
        load.wait()

    steps = groups // ROWS_STEP

    def mix_columns(step):
        rows = pl.ds(step * step_rows, step_rows)
        operand = jnp.concatenate([stem[0, rows, :], stem[1, rows, :]], 1)
        mixed = dot(operand, column_table).astype(BF16)
        pieces = []
        for index in range(ROWS_STEP):
            piece = mixed[index * row_order : (index + 1) * row_order]
            pieces.append(jnp.concatenate([piece[:, :width], piece[:, width:]], 0))
        return jnp.concatenate(pieces, 1)

    def mix_rows(step, mixed):
        result = dot(row_table, mixed)
        for index in range(ROWS_STEP):
            first = (step * ROWS_STEP + index) * heads
            spread[first : first + heads] = (
                result[:, index * width : (index + 1) * width]
                .reshape(heads, terms, width)
                .astype(BF16)
            )

    def mix(first, last, mixed):
        for step in range(first, last):
            later = mix_columns(step + 1) if step + 1 < steps else None
            mix_rows(step, mixed)
            mixed = later
        return mixed

    mixed = mix_columns(0)
    own = (iota((sub, order), 0) + me * sub == mode_labels[...]).astype(BF16)
    mode_real, mode_imag = dot(own, mode[0]), dot(own, mode[1])
    lane = iota((terms, span), 1)
    repeat = functools.reduce(
        jnp.logical_or,
        [lane == iota((terms, span), 0) + place * terms for place in range(TILE)],
    ).astype(BF16)
    mixed = mix(0, steps // 4, mixed)
    halves = [
        jnp.transpose(half).astype(BF16) for half in complex_rows(mode_real, mode_imag, 0)
    ]
    mixed = mix(steps // 4, steps // 2, mixed)
    blocks_of = jnp.concatenate(
        [dot(half, repeat).reshape(row_blocks, fold, span) for half in halves], 1
    )
    mixed = mix(steps // 2, 3 * steps // 4, mixed)
    lane = iota(blocks_of.shape, 2)
    for place in range(TILE):
        inside = (lane >= place * terms) & (lane < (place + 1) * terms)
        coeffs[place] = jnp.where(inside, blocks_of, 0.0).astype(BF16)
    final_table[0, :, :out_width] = final[0]
    final_table[0, :, out_width:] = final[1]
    final_table[1, :, :out_width] = -final[1]
    final_table[1, :, out_width:] = final[0]
    mix(3 * steps // 4, steps, mixed)

    for ask in asks:
        ask.wait_recv()
    to_scalars = pltpu.make_async_copy(asked, indices, index_sem)
    to_scalars.start()
    to_scalars.wait()

    def mode_products(first_slot, last_slot):
        first, last = first_slot * padded, last_slot * padded
        for start in range(first, last, TILE):
            left, right = [], []
            for place in range(TILE):
                slot, entry = (start + place) // padded, (start + place) % padded
                left.append(coeffs[place, indices[2 * slot + 1, entry]])
                right.append(spread[indices[2 * slot, entry]])
            partial[start * 2 * fold : (start + TILE) * 2 * fold, :] = dot(
                jnp.concatenate(left, 0), jnp.concatenate(right, 0)
            )

    def final_products(first_slot, last_slot):
        first, rows = first_slot * padded, (last_slot - first_slot) * padded
        pieces = [
            partial[pl.ds(first * 2 * fold + index, rows, stride=2 * fold), :].astype(BF16)
            for index in range(2 * fold)
        ]
        real = jnp.concatenate(pieces[:fold], 1)
        imag = jnp.concatenate(pieces[fold:], 1)
        return dot(real, final_table[0]) + dot(imag, final_table[1])

    gives = [
        pltpu.make_async_remote_copy(
            src_ref=outgoing.at[offset],
            dst_ref=incoming.at[offset],
            send_sem=give_send.at[offset],
            recv_sem=give_recv.at[offset],
            device_id=device(offset),
            device_id_type=pl.DeviceIdType.MESH,
        )
        for offset in range(1, peers)
    ]
    middle = peers // 2
    edges = [peers, middle + middle // 2, middle, 1, 0]
    chunks = list(zip(edges[1:], edges[:-1]))
    mode_products(*chunks[0])
    for index, (first, last) in enumerate(chunks):
        if index + 1 < len(chunks):
            mode_products(*chunks[index + 1])
        result = final_products(first, last)
        if first:
            outgoing[first:last] = result.reshape(last - first, padded, 2 * out_width).astype(BF16)
            for give in gives[first - 1 : last - 1]:
                give.start()
    answer = result
    for offset in reversed(range(1, peers)):
        gives[offset - 1].wait_recv()
        answer = answer + incoming[offset].astype(F32)
    answer = answer.astype(out_ref.dtype)
    out_ref[0, 0] = answer[:count, :out_width]
    out_ref[1, 0] = answer[:count, out_width:]
    for copy in asks + gives:
        copy.wait_send()


def fused(mode_size, group_size, padded, arguments):
    stem_slice, column, row, mode, final, row_labels, mode_labels, requests = arguments
    peers = mode_size * group_size
    row_count, width = stem_slice.shape[2:]
    order = mode.shape[1]
    sub = order // peers
    fold = final.shape[1] // width
    out_width = final.shape[2]
    count = requests.shape[1]
    total = peers * padded
    terms = 2 * sub
    span = terms * TILE
    row_labels = row_labels.reshape(1, -1)
    mode_labels = mode_labels.reshape(1, -1)
    dma = pltpu.SemaphoreType.DMA
    return pl.pallas_call(
        functools.partial(fused_kernel, mode_size, group_size),
        out_shape=pltpu.VMEM((2, 1, count, out_width), BF16),
        in_specs=[pl.BlockSpec(memory_space=pltpu.HBM)] * 8,
        out_specs=pl.BlockSpec(memory_space=pltpu.VMEM),
        scratch_shapes=[
            pltpu.VMEM((2, row_count, width), BF16),
            pltpu.VMEM(column.shape, BF16),
            pltpu.VMEM(row.shape, BF16),
            pltpu.VMEM(mode.shape, BF16),
            pltpu.VMEM(final.shape, BF16),
            pltpu.VMEM(row_labels.shape, jnp.int32),
            pltpu.VMEM(mode_labels.shape, jnp.int32),
            pltpu.VMEM(requests.shape, jnp.int32),
            pltpu.VMEM((2 * peers, width), jnp.int32),
            pltpu.SMEM((2 * peers, width), jnp.int32),
            pltpu.VMEM((row_count // sub, terms, width), BF16),
            pltpu.VMEM((TILE, order // fold, 2 * fold, span), BF16),
            pltpu.VMEM((2, fold * width, 2 * out_width), BF16),
            pltpu.VMEM((total * 2 * fold, width), F32),
            pltpu.VMEM((peers, padded, 2 * out_width), BF16),
            pltpu.VMEM((peers, padded, 2 * out_width), BF16),
            dma((7,)),
            dma,
            dma((2,)),
            dma((peers,)),
            dma((peers,)),
            dma((peers,)),
            dma((peers,)),
        ],
        compiler_params=pltpu.CompilerParams(
            collective_id=0, has_side_effects=True, vmem_limit_bytes=60 * 1024 * 1024
        ),
    )(stem_slice, column, row, mode, final, row_labels, mode_labels, requests)


def complex_table(weight):
    real_part = weight[0]
    imag_part = weight[1]
    return jnp.stack([jnp.stack([real_part, imag_part], 1), jnp.stack([-imag_part, real_part], 1)])


def relabel(weight, labels):
    label_count = labels.shape[0]
    onehot = (labels[:, None] == jnp.arange(label_count, dtype=jnp.int32)[None, :]).astype(
        jnp.float32
    )
    relabelled = jnp.einsum(
        "ji,zjn->zin", onehot, weight.astype(jnp.float32), precision=lax.Precision.HIGHEST
    )
    return complex_table(relabelled.astype(jnp.bfloat16))


def swapped(
    stem_slice,
    column_branch,
    row_branch,
    mode_branch,
    final_branch,
    row_labels,
    mode_labels,
    requests,
):
    local_block = stem_slice[:, 0]
    row_count = local_block.shape[1]
    col_width = local_block.shape[2]
    first_mixed = jnp.einsum(
        "zlc,zcwk->wlk",
        local_block,
        complex_table(column_branch),
        preferred_element_type=jnp.float32,
    ).astype(jnp.bfloat16)
    grouped = first_mixed.reshape(2, row_count // col_width, col_width, col_width)
    second = jnp.einsum(
        "zgjc,zjwk->wgkc",
        grouped,
        relabel(row_branch, row_labels),
        preferred_element_type=jnp.float32,
    ).astype(jnp.bfloat16)
    peer_count = lax.axis_size(("mode", "group"))
    order_size = mode_branch.shape[1]
    sub_rows = order_size // peer_count
    blocks = row_count // order_size
    mode_table = relabel(mode_branch, mode_labels).reshape(2, peer_count, sub_rows, 2, order_size)
    shaped = second.reshape(2, peer_count, blocks, sub_rows, col_width)
    mode_mixed = jnp.einsum(
        "zqhsc,zqswk->whkc",
        lax.all_to_all(shaped, ("mode", "group"), split_axis=1, concat_axis=1, tiled=True),
        mode_table,
        preferred_element_type=jnp.float32,
    ).astype(jnp.bfloat16)
    stem_rows = mode_mixed.reshape(2, row_count // 8, 8 * col_width)
    row_total = stem_rows.shape[1]
    wanted = requests[0]
    owner_index = wanted // row_total
    row_index = wanted - owner_index * row_total
    peer_ids = jnp.arange(peer_count, dtype=jnp.int32)
    onehot = (owner_index[:, None] == peer_ids[None, :]).astype(jnp.int32)
    slot_rank = jnp.sum((jnp.cumsum(onehot, axis=0) - onehot) * onehot, axis=1)
    flat_slot = owner_index * CAPACITY + slot_rank
    send_rows = (
        jnp.full((peer_count * CAPACITY,), -1, jnp.int32)
        .at[flat_slot]
        .set(row_index)
        .reshape(peer_count, CAPACITY)
    )
    asked_rows = lax.all_to_all(
        send_rows, ("mode", "group"), split_axis=0, concat_axis=0, tiled=True
    )
    safe_rows = jnp.maximum(asked_rows, 0).reshape(-1)
    final_table = complex_table(final_branch)
    results = jnp.einsum(
        "zlr,zrwk->wlk", stem_rows, final_table, preferred_element_type=jnp.float32
    ).astype(jnp.bfloat16)
    picked = jnp.take(results, safe_rows, axis=1).reshape(2, peer_count, CAPACITY, results.shape[2])
    returned = lax.all_to_all(picked, ("mode", "group"), split_axis=1, concat_axis=1, tiled=True)
    amplitudes = jnp.take(
        returned.reshape(2, peer_count * CAPACITY, results.shape[2]), flat_slot, axis=1
    )
    return amplitudes[:, None]


def per_device(mode_size, group_size, *arguments):
    stem_slice, _, row, mode, final, _, _, requests = arguments
    peers = mode_size * group_size
    row_count, width = stem_slice.shape[2:]
    padded = -(-requests.shape[1] // 16) * 16
    fits = (
        peers == TILE
        and padded <= width
        and row.shape[1] == width
        and mode.shape[1] % (16 * peers) == 0
        and row_count % (ROWS_STEP * width) == 0
        and 2 * peers * padded * final.shape[2] < stem_slice.size
    )
    if fits:
        return fused(mode_size, group_size, padded, arguments)
    return swapped(*arguments)


def solution(mesh):
    return jax.shard_map(
        functools.partial(per_device, mesh.shape["mode"], mesh.shape["group"]),
        mesh=mesh,
        in_specs=(
            P(None, ("cuts", "batch"), ("mode", "group"), None),
            P(),
            P(),
            P(),
            P(),
            P(),
            P(),
            P("batch", ("mode", "group")),
        ),
        out_specs=P(None, ("cuts", "batch"), ("mode", "group"), None),
        check_vma=False,
    )
```
